128 devices in a mesh: pipe: 4 (over z_hi, core), expert: 32 (over x, z_lo, y).
Axes of the slice: x: 4, y: 4, z: 4 (z_hi: 2, z_lo: 2; z = z_hi * 2 + z_lo), core: 2. Of those that a mesh axis runs over, the one named last changes fastest.
Arguments:
- activations: bfloat16 [4, 2, 2048, 7168], P('pipe', None, 'expert'), may hold values from -6 to 6
- expert_ids: int32 [4, 2, 2048, 2], P('pipe', None, 'expert'), may hold values from 0 to 7, all different within a row; in each aligned block of 64 rows (0 to 63, 64 to 127, ..., all dimensions but the last counted through in order) at most 20 rows name the same one
- gate_values: float32 [4, 2, 2048, 2], P('pipe', None, 'expert'), may hold values from 0.25 to 1
- gate_weight: bfloat16 [4, 2, 7168, 8192], P('pipe', None, None, 'expert'), may hold values from -0.0625 to 0.0625
- up_weight: bfloat16 [4, 2, 7168, 8192], P('pipe', None, None, 'expert'), may hold values from -0.0625 to 0.0625
- down_weight: bfloat16 [4, 2, 8192, 7168], P('pipe', None, 'expert'), may hold values from -0.1875 to 0.1875
Outputs:
- moved: bfloat16 [4, 2, 2048, 7168], P('pipe', None, 'expert')
The draws below stay inside these ranges and needn't reach their ends.
Inputs may be any that keep to these rules, and one draw needn't show every extreme that they name: `expert_ids`: each row names 2 different experts; among the 64 rows of one index of expert for one rank and section, no expert is named by more than 20 rows, and in some such blocks one expert is named by exactly 20.
All inputs are finite; a program needn't handle non-finite values.
Results may differ from the reference program's by a relative error of at most 0.0041.
Values may be sent and summed in bfloat16 or wider, within the bound.
No kernel may reach another device: no remote copies, remote signals or barrier semaphores. Data moves between devices by JAX's collectives and lax.ppermute only.
A program may use at most 192 MiB of HBM per device.

```python
import math
import jax
import jax.numpy as jnp
import numpy as np
from jax import lax

D = 7168
FW = 1024
EXPERTS = 8
TOPK = 2
TOK = 64
RANKS = 4
SPLIT = 4
HID_DEV = 256
CAP = 20
TOKENS = 2048


def level_of(stream_key, extent, split, smallest, top_value):
    def one(position, parts):
        draws = jax.random.uniform(jax.random.fold_in(jax.random.fold_in(stream_key, 6), position), (parts,), jnp.float32, smallest / len(split), top_value / len(split))
        return jnp.repeat(jnp.exp(draws), extent[position] // parts).reshape((-1,) + (1,) * (len(extent) - position - 1))

    loudness = one(*split[0])
    for cut in split[1:]:
        loudness = loudness * one(*cut)
    return loudness


def routed_block(stream_key, own, number, rows, amount, top, bound, slope):
    sequence = jax.random.permutation(stream_key, amount)
    heavy_load, common = load_shares(amount, rows * top, bound, slope, True), load_shares(amount, rows * top, bound, slope, False)
    places = jnp.arange(amount)

    def named(lengths, rotation):
        used = int((lengths > 0).sum())
        fixed = max(1, used // 4)
        shifted = fixed + (places - fixed + rotation * (used - fixed)) % max(1, amount - fixed)
        return jnp.zeros((amount,), jnp.int32).at[sequence[jnp.where(places < fixed, places, shifted)]].set(jnp.asarray(lengths, jnp.int32))

    lengths = jnp.where(number % 4 == 0, named(heavy_load, number // 4), named(common, number - number // 4 - 1))
    mixed = jax.random.permutation(jax.random.fold_in(own, 3), amount)
    donor, taker = mixed[0:amount // 2 * 2:2], mixed[1:amount // 2 * 2:2]
    margin = jnp.minimum(lengths[donor] - 1, bound - lengths[taker]) // 2
    margin = jnp.where((donor == sequence[0]) | (taker == sequence[0]) | (lengths[taker] == 0), 0, jnp.maximum(margin, 0))
    shifted = jax.random.randint(jax.random.fold_in(own, 4), (amount // 2,), 0, 1 << 20) % (margin + 1)
    lengths = lengths.at[donor].add(-shifted).at[taker].add(shifted)
    items = jnp.searchsorted(jnp.cumsum(lengths), jnp.arange(rows * top), side="right").astype(jnp.int32)
    grid = items.reshape(top, rows).T
    grid = grid[jax.random.permutation(jax.random.fold_in(own, 1), rows)]
    rotation = jax.random.randint(jax.random.fold_in(own, 2), (rows, 1), 0, top)
    return jnp.take_along_axis(grid, (jnp.arange(top)[None, :] + rotation) % top, axis=1)


def load_shares(count, total, reach, slope, full):
    weights = [(1 << 20) // math.isqrt(standing ** slope) + 1 for standing in range(1, count + 1)]
    largest = reach if full else min(reach, max(-(-total // count), total * weights[0] // sum(weights)))
    least = 1 if total - largest >= count - 1 else 0
    given, rest = [largest] + [least] * (count - 1), total - largest - least * (count - 1)
    while rest > 0:
        candidates = [i for i in range(1, count) if given[i] < largest] or [i for i in range(1, count) if given[i] < reach]
        pool, left = sum([weights[i] for i in candidates]), rest
        for i in candidates:
            addition = min(reach - given[i], max(1, left * weights[i] // pool), rest)
            given[i] = given[i] + addition
            rest = rest - addition
    return np.array(given)


def gaussian(rng, extent, width, bound, split=(), kind=jnp.bfloat16):
    array = jax.random.normal(rng, extent, jnp.float32) * width
    if len(split) > 0:
        array = level_of(rng, extent, split, -0.22, 0.18) * array
    return jnp.clip(array, min=-bound, max=bound).astype(kind)


def setup_inputs(seed: int = 0) -> dict:
    key_of = jax.random.split(jax.random.key(seed), 7)
    activations = gaussian(key_of[0], (RANKS, 2, TOKENS, D), 1.0, 6.0, ((0, 4), (2, 32)))
    expert_ids_keys = jax.random.split(jax.random.fold_in(key_of[1], 1), RANKS * 2 * TOKENS // TOK)
    expert_ids_turns = jax.random.permutation(jax.random.fold_in(key_of[1], 3), RANKS * 2 * TOKENS // TOK)
    expert_ids = jax.vmap(lambda own, number: routed_block(jax.random.fold_in(key_of[1], 2), own, number, TOK, EXPERTS, TOPK, CAP, 2))(expert_ids_keys, expert_ids_turns).reshape((RANKS, 2, TOKENS, TOPK))
    gate_values = jnp.clip(0.25 + 0.75 * jax.random.uniform(key_of[2], (RANKS, 2, TOKENS, TOPK), jnp.float32) ** level_of(key_of[2], (RANKS, 2, TOKENS, TOPK), ((0, 4), (2, 32)), -0.2, 0.2), 0.25, 1.0)
    gate_weight = gaussian(key_of[3], (RANKS, 2, D, EXPERTS * FW), D ** -0.5, 0.0625, ((0, 4), (3, 32)))
    up_weight = gaussian(key_of[4], (RANKS, 2, D, EXPERTS * FW), D ** -0.5, 0.0625, ((0, 4), (3, 32)))
    down_weight = gaussian(key_of[5], (RANKS, 2, EXPERTS * FW, D), FW ** -0.5, 0.1875, ((0, 4), (2, 32)))
    return {"activations": activations, "expert_ids": expert_ids, "gate_values": gate_values, "gate_weight": gate_weight, "up_weight": up_weight, "down_weight": down_weight}


def take_rows(table_rows, row_index):
    return table_rows[row_index]


def expert_apply(operands):
    token_rows, gate_matrix, up_matrix, down_matrix = operands
    gate_out = jnp.dot(token_rows, gate_matrix, preferred_element_type=jnp.float32)
    up_out = jnp.dot(token_rows, up_matrix, preferred_element_type=jnp.float32)
    hidden = (jax.nn.silu(gate_out) * up_out).astype(jnp.bfloat16)
    row_count = token_rows.shape[0]
    hidden_blocks = hidden.reshape(row_count, SPLIT, HID_DEV).astype(jnp.float32)
    down_blocks = down_matrix.reshape(SPLIT, HID_DEV, D).astype(jnp.float32)
    partial_value = jnp.einsum("rjh,jhd->jrd", hidden_blocks, down_blocks).astype(jnp.bfloat16)
    partial_value = lax.optimization_barrier(partial_value)
    return jnp.sum(partial_value.astype(jnp.float32), axis=0)


def moe_section(token_rows, chosen_ids, chosen_weights, gate_matrix, up_matrix, down_matrix):
    blocks_count = TOKENS // TOK
    picks_total = TOK * TOPK
    chosen = chosen_ids.reshape(blocks_count, picks_total).astype(jnp.int32)
    onehot = (chosen[:, :, None] == jnp.arange(EXPERTS, dtype=jnp.int32)[None, None, :]).astype(jnp.int32)
    rank_within = jnp.sum((jnp.cumsum(onehot, axis=1) - 1) * onehot, axis=2).astype(jnp.int32)
    slot_index = (chosen * CAP + rank_within).astype(jnp.int32)
    source = jnp.full((blocks_count, EXPERTS * CAP), picks_total, jnp.int32)
    pick_numbers = jnp.broadcast_to(jnp.arange(picks_total, dtype=jnp.int32)[None, :], (blocks_count, picks_total))
    source = source.at[jnp.arange(blocks_count, dtype=jnp.int32)[:, None], slot_index].set(pick_numbers)
    padded = jnp.concatenate([token_rows.reshape(blocks_count, TOK, D), jnp.zeros((blocks_count, 1, D), token_rows.dtype)], axis=1)
    gathered = jax.vmap(take_rows)(padded, (source // TOPK).astype(jnp.int32))
    grouped = gathered.reshape(blocks_count, EXPERTS, CAP, D).transpose(1, 0, 2, 3).reshape(EXPERTS, blocks_count * CAP, D)
    gate_split = gate_matrix.reshape(D, EXPERTS, FW).transpose(1, 0, 2)
    up_split = up_matrix.reshape(D, EXPERTS, FW).transpose(1, 0, 2)
    down_split = down_matrix.reshape(EXPERTS, FW, D)
    outputs = lax.map(expert_apply, (grouped, gate_split, up_split, down_split))
    returned = outputs.reshape(EXPERTS, blocks_count, CAP, D).transpose(1, 0, 2, 3).reshape(blocks_count, EXPERTS * CAP, D)
    picked = jax.vmap(take_rows)(returned, slot_index)
    weighted = picked * chosen_weights.reshape(blocks_count, picks_total)[:, :, None].astype(jnp.float32)
    combined = jnp.sum(weighted.reshape(TOKENS, TOPK, D), axis=1) + token_rows.astype(jnp.float32)
    return combined.astype(jnp.bfloat16)


def reference(activations, expert_ids, gate_values, gate_weight, up_weight, down_weight):
    results = []
    for rank_index in range(RANKS):
        pair = []
        for slot_number in range(2):
            pair.append(moe_section(activations[rank_index, slot_number], expert_ids[rank_index, slot_number],
                                  gate_values[rank_index, slot_number], gate_weight[rank_index, slot_number],
                                  up_weight[rank_index, slot_number], down_weight[rank_index, slot_number]))
        results.append(pair)
    first_slots = [results[0][1]] + [results[rank_index - 1][0] for rank_index in range(1, RANKS)]
    second_slots = [results[rank_index + 1][1] for rank_index in range(RANKS - 1)] + [results[RANKS - 1][0]]
    return jnp.stack([jnp.stack([first_slots[rank_index], second_slots[rank_index]]) for rank_index in range(RANKS)])
```

```python
import jax
import jax.numpy as jnp
from jax import lax
from jax.sharding import Mesh, PartitionSpec as P

EXPERTS = 8
CAP = 20
BF = jnp.bfloat16
F32 = jnp.float32


def dot(a, b):
    return jnp.dot(a, b, preferred_element_type=F32)


def slots(ids):
    tokens = ids.shape[0]
    chose = jnp.any(ids[:, :, None] == jnp.arange(EXPERTS, dtype=jnp.int32), axis=1)
    before = jnp.tril(jnp.ones((tokens, tokens), BF), -1)
    rank = dot(before, chose.astype(BF)).astype(jnp.int32)
    return jnp.where(chose, rank, -1)


def dispatch_matrix(ids):
    slot = slots(ids)
    return (slot.T[:, None, :] == jnp.arange(CAP, dtype=jnp.int32)[None, :, None]).astype(BF)


def combine_matrix(ids, gates):
    slot = jax.vmap(slots)(ids)
    weight = jnp.sum(
        jnp.where(ids[..., None] == jnp.arange(EXPERTS, dtype=jnp.int32), gates[..., None], 0.0), axis=2
    )
    group = ids.shape[0]
    hit = slot[:, :, :, None, None] == jnp.arange(CAP, dtype=jnp.int32)
    same = jnp.arange(group)[:, None, None, None, None] == jnp.arange(group)[None, None, None, :, None]
    return jnp.where(hit & same, weight[:, :, :, None, None], 0.0)


def local(activations, expert_ids, gate_values, gate_weight, up_weight, down_weight):
    tokens, width = activations.shape[2:]
    group = lax.axis_size("y")
    part = width // group
    pipe_index = lax.axis_index("pipe")
    last = lax.axis_size("pipe") - 1

    routing = jnp.concatenate([expert_ids[0].astype(F32), gate_values[0]], axis=2)
    routing = lax.all_gather(routing, "y", axis=0)

    sums = []
    for s in range(2):
        rows = activations[0, s]
        outgoing = dot(dispatch_matrix(expert_ids[0, s]).reshape(EXPERTS * CAP, tokens), rows).astype(BF)
        arrived = lax.all_to_all(
            outgoing.reshape(EXPERTS, CAP, width), ("x", "z"), split_axis=0, concat_axis=0, tiled=True
        )
        gathered = lax.all_gather(arrived.reshape(EXPERTS * CAP, width), "y", axis=0, tiled=True)
        gate_out = dot(gathered, gate_weight[0, s])
        up_out = dot(gathered, up_weight[0, s])
        hidden = (jax.nn.silu(gate_out) * up_out).astype(BF)
        block = hidden.shape[1]
        hidden = hidden.reshape(group, EXPERTS, CAP, block).transpose(1, 0, 2, 3)
        hidden = lax.all_gather(hidden.reshape(-1, block), "y", axis=0)
        hidden = jnp.concatenate([hidden[j] for j in range(group)], axis=1)
        down = lax.all_to_all(
            down_weight[0, s].reshape(block, group, part).transpose(1, 0, 2),
            "y", split_axis=0, concat_axis=0, tiled=True,
        ).reshape(group * block, part)
        out = dot(hidden, down).astype(BF).reshape(EXPERTS, group * CAP, part)
        back = lax.all_to_all(out, ("x", "z"), split_axis=0, concat_axis=0, tiled=True)
        back = back.reshape(EXPERTS * group * CAP, part)
        mix = combine_matrix(routing[:, s, :, :2].astype(jnp.int32), routing[:, s, :, 2:])
        mix = mix.reshape(group * tokens, EXPERTS * group * CAP)
        high = lax.reduce_precision(mix, 8, 7)
        total = dot(high.astype(BF), back) + dot((mix - high).astype(BF), back)
        total = total.astype(BF).reshape(group, tokens, part)
        total = lax.all_to_all(total, "y", split_axis=0, concat_axis=0, tiled=True)
        total = total.transpose(1, 0, 2).reshape(tokens, width).astype(F32)
        sums.append((rows.astype(F32) + total).astype(BF))

    size = lax.axis_size("pipe")
    ahead = lax.ppermute(sums[0], "pipe", [(i, i + 1) for i in range(size - 1)])
    behind = lax.ppermute(sums[1], "pipe", [(i + 1, i) for i in range(size - 1)])
    first = jnp.where(pipe_index == 0, sums[1], ahead)
    second = jnp.where(pipe_index == last, sums[0], behind)
    return jnp.stack([first, second])[None]


def solution(mesh):
    pipe, expert = mesh.devices.shape
    group = 4
    split = Mesh(mesh.devices.reshape(pipe, 4, 2, group), ("pipe", "x", "z", "y"))
    wide = ("x", "z", "y")
    return jax.shard_map(
        local,
        mesh=split,
        in_specs=(
            P("pipe", None, wide, None),
            P("pipe", None, wide, None),
            P("pipe", None, wide, None),
            P("pipe", None, None, wide),
            P("pipe", None, None, wide),
            P("pipe", None, wide, None),
        ),
        out_specs=P("pipe", None, wide, None),
        check_vma=False,
    )
```

```python
import jax
import jax.numpy as jnp
from jax import lax
from jax.sharding import Mesh, PartitionSpec as P

EXPERTS = 8
CAP = 20
GROUP = 4
BF = jnp.bfloat16
F32 = jnp.float32


def dot(a, b):
    return jnp.dot(a, b, preferred_element_type=F32)


def after(value, *earlier):
    return lax.optimization_barrier((value, *earlier))[0]


def shift(value, steps):
    return lax.ppermute(value, "y", [(i, (i + steps) % GROUP) for i in range(GROUP)])


def exchange(value):
    return lax.all_to_all(value, ("x", "z"), split_axis=0, concat_axis=0, tiled=True)


def slots(ids):
    tokens = ids.shape[0]
    chose = jnp.any(ids[:, :, None] == jnp.arange(EXPERTS, dtype=jnp.int32), axis=1)
    before = jnp.tril(jnp.ones((tokens, tokens), BF), -1)
    rank = dot(before, chose.astype(BF)).astype(jnp.int32)
    return jnp.where(chose, rank, -1)


def in_order(pieces, axis, y):
    size = pieces[0].shape[axis]
    joined = jnp.concatenate(pieces[::-1] + pieces[:0:-1], axis=axis)
    return lax.dynamic_slice_in_dim(joined, (GROUP - 1 - y) * size, GROUP * size, axis)


def down_parts(down, y):
    part = down.shape[1] // GROUP
    cut = [lax.dynamic_slice_in_dim(down, (y + k) % GROUP * part, part, 1) for k in range(GROUP)]
    return [cut[0]] + [shift(cut[k], k) for k in range(1, GROUP)]


def hidden_of(rows, gate, up):
    return (jax.nn.silu(dot(rows, gate)) * dot(rows, up)).astype(BF)


def finish(hidden, parts, slot, weight, y):
    units = [hidden] + [shift(hidden, k) for k in range(1, GROUP)]
    out = dot(jnp.concatenate(units, axis=1), jnp.concatenate(parts, axis=0)).astype(BF)
    part = out.shape[1]
    back = exchange(out.reshape(EXPERTS, GROUP * CAP, part)).reshape(EXPERTS * GROUP * CAP, part)
    tokens = slot.shape[1]
    hit = slot[:, :, :, None, None] == jnp.arange(CAP, dtype=jnp.int32)
    near = jnp.arange(GROUP)
    same = near[:, None, None, None, None] == near[None, None, None, :, None]
    mix = jnp.where(hit & same, weight[:, :, :, None, None], 0.0).reshape(GROUP * tokens, -1)
    high = lax.reduce_precision(mix, 8, 7)
    total = (dot(high.astype(BF), back) + dot((mix - high).astype(BF), back)).astype(BF)
    total = total.reshape(GROUP, tokens, part)
    mine = [lax.dynamic_index_in_dim(total, (y + k) % GROUP, 0, False) for k in range(GROUP)]
    return in_order([mine[0]] + [shift(mine[k], k) for k in range(1, GROUP)], 1, y)


def local(activations, expert_ids, gate_values, gate_weight, up_weight, down_weight):
    tokens, width = activations.shape[2:]
    half = width // 2
    y = lax.axis_index("y")
    pipe_index = lax.axis_index("pipe")
    last = lax.axis_size("pipe") - 1
    first_rows, second_rows = activations[0, 0], activations[0, 1]

    near = [second_rows] + [shift(second_rows, k) for k in range(1, GROUP)]

    slot = slots(expert_ids[0, 0])
    choose = (slot.T[:, None, :] == jnp.arange(CAP, dtype=jnp.int32)[None, :, None]).astype(BF)
    both = jnp.eye(2, dtype=BF)
    choose = (choose[:, None, :, None, :] * both[None, :, None, :, None]).reshape(EXPERTS * 2 * CAP, 2 * tokens)
    halves = jnp.concatenate([first_rows[:, :half], first_rows[:, half:]], axis=0)
    arrived = exchange(dot(choose, halves).astype(BF).reshape(EXPERTS, 2 * CAP, half))
    arrived = arrived.reshape(EXPERTS * 2 * CAP, half)
    order = jnp.arange(EXPERTS * CAP, dtype=jnp.int32)
    source = order // CAP * 2 * CAP + order % CAP
    pick = [
        (source[:, None] + h * CAP == jnp.arange(EXPERTS * 2 * CAP, dtype=jnp.int32)).astype(BF) for h in range(2)
    ]
    arrived = jnp.concatenate([dot(pick[h], arrived).astype(BF) for h in range(2)], axis=1)

    routing = jnp.concatenate([expert_ids[0].astype(F32), gate_values[0]], axis=2)
    routing = lax.all_gather(routing, "y", axis=0)
    ids = routing[..., :2].astype(jnp.int32)
    gates = routing[..., 2:]
    slot = jax.vmap(jax.vmap(slots))(ids)
    weight = jnp.sum(
        jnp.where(ids[..., None] == jnp.arange(EXPERTS, dtype=jnp.int32), gates[..., None], 0.0), axis=3
    )

    behind = jnp.concatenate(near, axis=0)
    slot_behind = jnp.stack([lax.dynamic_index_in_dim(slot[:, 1], (y - k) % GROUP, 0, False) for k in range(GROUP)])
    owner = (y - jnp.arange(GROUP, dtype=jnp.int32)) % GROUP
    hit = slot_behind.transpose(2, 0, 1)[:, None, None] == jnp.arange(CAP, dtype=jnp.int32)[:, None, None]
    same = jnp.arange(GROUP, dtype=jnp.int32)[:, None] == owner
    choose = (hit & same[None, :, None, :, None]).astype(BF).reshape(EXPERTS * GROUP * CAP, GROUP * tokens)
    chosen = dot(choose, behind).astype(BF).reshape(EXPERTS, GROUP * CAP, width)
    chosen = exchange(chosen).reshape(EXPERTS * GROUP * CAP, width)

    parts = [down_parts(after(down_weight[0, 0], behind), y)]

    ahead, back = shift(arrived, 1), shift(arrived, -1)
    middle = EXPERTS * CAP // 2
    far = [shift(ahead[:middle], 1), shift(back[middle:], -1)]
    parts.append(down_parts(after(down_weight[0, 1], ahead, back), y))
    gate, up = gate_weight[0, 0], up_weight[0, 0]
    pieces = [hidden_of(rows, gate, up) for rows in (arrived, ahead, jnp.concatenate(far, axis=0), back)]
    block = pieces[0].shape[1]
    hidden = in_order([piece[None] for piece in pieces], 0, y)
    hidden = hidden.reshape(GROUP, EXPERTS, CAP, block).transpose(1, 0, 2, 3).reshape(-1, block)
    sums = [finish(hidden, parts[0], slot[:, 0], weight[:, 0], y)]

    hidden = hidden_of(chosen, gate_weight[0, 1], up_weight[0, 1])
    sums.append(finish(hidden, parts[1], slot[:, 1], weight[:, 1], y))

    results = [
        (rows.astype(F32) + total.astype(F32)).astype(BF)
        for rows, total in zip((first_rows, second_rows), sums)
    ]
    size = lax.axis_size("pipe")
    ahead = lax.ppermute(results[0], "pipe", [(i, i + 1) for i in range(size - 1)])
    behind = lax.ppermute(results[1], "pipe", [(i + 1, i) for i in range(size - 1)])
    first = jnp.where(pipe_index == 0, results[1], ahead)
    second = jnp.where(pipe_index == last, results[0], behind)
    return jnp.stack([first, second])[None]


def solution(mesh):
    pipe = mesh.devices.shape[0]
    split = Mesh(mesh.devices.reshape(pipe, 4, 2, GROUP), ("pipe", "x", "z", "y"))
    wide = ("x", "z", "y")
    return jax.shard_map(
        local,
        mesh=split,
        in_specs=(
            P("pipe", None, wide, None),
            P("pipe", None, wide, None),
            P("pipe", None, wide, None),
            P("pipe", None, None, wide),
            P("pipe", None, None, wide),
            P("pipe", None, wide, None),
        ),
        out_specs=P("pipe", None, wide, None),
        check_vma=False,
    )
```

```python
import functools

import jax
import jax.numpy as jnp
import numpy as np
from jax import lax
from jax.experimental import pallas as pl
from jax.experimental.pallas import tpu as pltpu
from jax.sharding import Mesh, PartitionSpec as P

EXPERTS = 8
CAP = 20
GROUP = 4
PAIR = 2
LANES = 128
STRIDE = 64
BF = jnp.bfloat16
F32 = jnp.float32


def dot(a, b):
    return jnp.dot(a, b, preferred_element_type=F32)


def dot_t(a, b):
    return lax.dot_general(a, b, (((1,), (1,)), ((), ())), preferred_element_type=F32)


def tie(*values):
    anywhere = [pl.BlockSpec(memory_space=pl.ANY)] * len(values)
    return pl.pallas_call(
        lambda *refs: None,
        out_shape=[jax.ShapeDtypeStruct(value.shape, value.dtype) for value in values],
        in_specs=anywhere,
        out_specs=anywhere,
        input_output_aliases={i: i for i in range(len(values))},
    )(*values)


def call(kernel, out_shape, grid, in_specs, out_specs, scratch=(), moved=0):
    return pl.pallas_call(
        kernel,
        cost_estimate=pl.CostEstimate(flops=0, transcendentals=0, bytes_accessed=moved),
        out_shape=out_shape,
        grid_spec=pltpu.PrefetchScalarGridSpec(
            num_scalar_prefetch=1, grid=grid, in_specs=in_specs, out_specs=out_specs, scratch_shapes=scratch
        ),
        compiler_params=pltpu.CompilerParams(vmem_limit_bytes=48 * 1024 * 1024),
    )


def shape(*dims):
    return jax.ShapeDtypeStruct(dims, BF)


def whole(value):
    return pl.BlockSpec(value.shape, lambda *_: (0,) * len(value.shape))


def columns_of(rows, tile):
    return pl.BlockSpec((rows, tile), lambda j, y: (0, j))


def shift(value, steps):
    return lax.ppermute(value, "y", [(i, (i + steps) % GROUP) for i in range(GROUP)])


def shifts(pieces):
    return [shift(pieces[k - 1], k) for k in range(1, GROUP)]


def spread(value):
    return [shift(value, k) for k in range(1, GROUP)]


def exchange(value):
    return lax.all_to_all(value, ("x", "z"), split_axis=0, concat_axis=0, tiled=True)


def packed(ids, gates):
    high = lax.reduce_precision(gates, 8, 7)
    middle = lax.reduce_precision(gates - high, 8, 7)
    return jnp.concatenate([ids.astype(F32), high, middle, gates - high - middle], axis=-1).astype(BF)


def unpacked(columns):
    top = columns.shape[-1] // 4
    columns = [columns[:, i * top : (i + 1) * top].astype(F32) for i in range(4)]
    return columns[0].astype(jnp.int32), (columns[1] + columns[2]) + columns[3]


def keys(ids, before, place):
    named = [ids[:, k : k + 1] == jnp.arange(LANES, dtype=jnp.int32) for k in range(ids.shape[1])]
    chose = functools.reduce(jnp.logical_or, named)
    rank = dot(before, chose.astype(BF))
    return jnp.where(chose, rank + place, -1.0).astype(BF), named


def expert_rows(per_expert):
    return np.asarray(np.arange(EXPERTS * per_expert)[:, None] // per_expert == np.arange(LANES), dtype=BF)


def codes(places):
    return np.asarray([STRIDE * place + c for _ in range(EXPERTS) for place in places for c in range(CAP)], np.float32)


def unfold(y, pick, value):
    rows, half = pick.shape[1], value.shape[1]

    def kernel(y_ref, pick_ref, value_ref, out_ref):
        out_ref[...] = dot(pick_ref[0], value_ref[...]).astype(BF)

    return call(
        kernel,
        shape(rows, 2 * half),
        (2,),
        [pl.BlockSpec((1,) + pick.shape[1:], lambda h, y: (h, 0, 0)), whole(value)],
        columns_of(rows, half),
    )(y, pick, value)


def quarters(y, down, section, runs):
    depth, part = down.shape[2], down.shape[3] // GROUP // runs
    count = (GROUP - 1) * runs

    def kernel(y_ref, down_ref, *refs):
        for i in range(count):

            @pl.when(pl.program_id(0) == i)
            def _():
                refs[i][...] = down_ref[0, 0]

    def column(i, y):
        return (0, section, 0, lax.rem(y[0] + i // runs + 1, GROUP) * runs + lax.rem(i, runs))

    cuts = call(
        kernel,
        [shape(depth, part)] * count,
        (count,),
        [pl.BlockSpec((1, 1, depth, part), column)],
        [pl.BlockSpec((depth, part), lambda k, y: (0, 0))] * count,
    )(y, down)
    return [cuts[run::runs] for run in range(runs)]


def hidden_of(y, rows, gate, up, section):
    width, block = gate.shape[2:]
    total = sum(run.shape[0] for run in rows)
    tile = 1024
    steps = width // tile

    def kernel(y_ref, gate_ref, up_ref, *refs):
        *runs, out_ref, gate_sum, up_sum = refs
        step = pl.program_id(0)

        @pl.when(step == 0)
        def _():
            gate_sum[...] = jnp.zeros_like(gate_sum)
            up_sum[...] = jnp.zeros_like(up_sum)

        value = jnp.concatenate([run[...] for run in runs], axis=0) if len(runs) > 1 else runs[0][...]
        gate_sum[...] += dot(value, gate_ref[0, 0])
        up_sum[...] += dot(value, up_ref[0, 0])

        @pl.when(step == steps - 1)
        def _():
            out_ref[...] = (jax.nn.silu(gate_sum[...]) * up_sum[...]).astype(BF)

    weights = pl.BlockSpec((1, 1, tile, block), lambda j, y: (0, section, j, 0))
    return call(
        kernel,
        shape(total, block),
        (steps,),
        [weights, weights] + [columns_of(run.shape[0], tile) for run in rows],
        pl.BlockSpec((total, block), lambda j, y: (0, 0)),
        [pltpu.VMEM((total, block), F32)] * 2,
        moved=20 * 2**20,
    )(y, gate, up, *rows)


def arrange(y, target, pieces):
    block = pieces[0].shape[1]
    rows = target.shape[1]

    def kernel(y_ref, target_ref, *refs):
        stacked = jnp.concatenate([ref[...] for ref in refs[:-1]], axis=0)
        moved = lax.broadcasted_iota(jnp.int32, (rows, rows), 0) == target_ref[...]
        refs[-1][...] = dot(moved.astype(F32).astype(BF), stacked).astype(BF)

    return call(
        kernel,
        shape(rows, block),
        (1,),
        [whole(target)] + [whole(piece) for piece in pieces],
        pl.BlockSpec((rows, block), lambda j, y: (0, 0)),
    )(y, target, *pieces)


def project(y, units, parts, down, section):
    rows, depth = units[0].shape
    part = sum(group[0].shape[1] for group in parts)
    tile = part // 2
    runs = len(parts)
    flat = [value for group in parts for value in group]

    def kernel(y_ref, *refs):
        *refs, out_ref, joined = refs
        step = pl.program_id(0)

        @pl.when(step == 0)
        def _():
            for k in range(GROUP):
                joined[:, k * depth : (k + 1) * depth] = refs[k][...]

        own, others = refs[GROUP], refs[GROUP + 1 :]
        for run in range(runs):

            @pl.when(step // (2 // runs) == run)
            def _():
                mine = others[run * (GROUP - 1) : (run + 1) * (GROUP - 1)]
                matrix = jnp.concatenate([own[0, 0], *(ref[...] for ref in mine)], axis=0)
                out_ref[...] = dot(joined[...], matrix).astype(BF)

    own = pl.BlockSpec((1, 1, depth, tile), lambda j, y: (0, section, 0, y[0] * 2 + j))
    others = [columns_of(depth, tile) if runs == 1 else whole(value) for value in flat]
    out = call(
        kernel,
        shape(rows, part),
        (2,),
        [whole(unit) for unit in units] + [own] + others,
        columns_of(rows, tile),
        [pltpu.VMEM((rows, GROUP * depth), BF)],
        moved=20 * 2**20,
    )(y, *units, down, *flat)
    return out.reshape(EXPERTS, GROUP * CAP, part)


def combine(y, back, key, weight):
    part, tile = back.shape[2], 896
    back = back.reshape(-1, part)
    tokens = key.shape[0] // GROUP
    onehot = expert_rows(GROUP * CAP)
    code = codes(range(GROUP))[None]
    high = lax.reduce_precision(weight, 8, 7)
    weights = [high.astype(BF), (weight - high).astype(BF)]

    def kernel(y_ref, key_ref, high_ref, low_ref, onehot_ref, code_ref, back_ref, *refs):
        expand = onehot_ref[...]
        hit = dot_t(key_ref[...], expand) == code_ref[...]
        total = 0.0
        for ref in (high_ref, low_ref):
            mix = jnp.where(hit, dot_t(ref[...], expand), 0.0).astype(BF)
            total += dot(mix, back_ref[...])
        total = total.astype(BF)
        for k in range(GROUP):
            refs[k][...] = total[k * tokens : (k + 1) * tokens]

    return call(
        kernel,
        [shape(tokens, part)] * GROUP,
        (part // tile,),
        [whole(value) for value in (key, *weights, onehot, code)] + [columns_of(back.shape[0], tile)],
        [columns_of(tokens, tile)] * GROUP,
    )(y, key, *weights, onehot, code, back)


def home(y, totals, rows):
    pieces = [totals[0], *shifts(totals[1:])]
    tokens, part = totals[0].shape

    def kernel(y_ref, rows_ref, *refs):
        for k in range(GROUP):

            @pl.when(pl.program_id(0) == k)
            def _():
                refs[-1][...] = (rows_ref[...].astype(F32) + refs[k][...].astype(F32)).astype(BF)

    quarter = pl.BlockSpec((tokens, part), lambda k, y: (0, lax.rem(y[0] + GROUP - k, GROUP)))
    return call(
        kernel,
        shape(*rows.shape),
        (GROUP,),
        [quarter] + [whole(piece) for piece in pieces],
        quarter,
    )(y, rows, *pieces)


def local(activations, expert_ids, gate_values, gate_weight, up_weight, down_weight):
    tokens, width = activations.shape[2:]
    top = expert_ids.shape[3]
    half = width // 2
    index = lax.axis_index("y").astype(jnp.int32)
    y = index.reshape(1)
    pipe_index = lax.axis_index("pipe")
    last = lax.axis_size("pipe") - 1
    first_rows, second_rows = activations[0, 0], activations[0, 1]

    before = np.asarray(np.tril(np.ones((tokens, tokens)), -1), dtype=BF)
    key, _ = keys(expert_ids[0, 0], before, 0.0)
    key = jnp.concatenate([key, jnp.where(key < 0, key, key + STRIDE)], axis=0)
    choose = (dot_t(expert_rows(2 * CAP), key) == codes(range(2))[:, None]).astype(BF)
    halves = jnp.concatenate([first_rows[:, :half], first_rows[:, half:]], axis=0)
    outgoing = dot(choose, halves).astype(BF).reshape(EXPERTS, 2 * CAP, half)
    routing = [packed(expert_ids[0, s], gate_values[0, s]) for s in range(2)]
    routing = jnp.concatenate([*routing, jnp.zeros((tokens, LANES - 8 * top), BF)], axis=1)
    arrived = exchange(outgoing)

    near = spread(second_rows)
    routing = jnp.concatenate([routing, *spread(routing)], axis=0)
    order = np.arange(EXPERTS * CAP)
    source = order // CAP * 2 * CAP + order % CAP + np.arange(2)[:, None] * CAP
    pick = np.asarray(source[:, :, None] == np.arange(EXPERTS * 2 * CAP), dtype=BF)
    arrived = unfold(y, pick, arrived.reshape(EXPERTS * 2 * CAP, half))
    (cuts0,), (cuts1,) = [quarters(y, down_weight, s, 1) for s in range(2)]

    owner = jnp.bitwise_and(index - np.arange(GROUP * tokens, dtype=np.int32)[:, None] // tokens, GROUP - 1)
    before = np.asarray(np.kron(np.eye(GROUP), np.tril(np.ones((tokens, tokens)), -1)), dtype=BF)
    key, weight = [], []
    for s in range(2):
        ids, gates = unpacked(routing[:, 4 * top * s : 4 * top * (s + 1)])
        found, named = keys(ids, before, (owner * STRIDE).astype(F32))
        key.append(found)
        weight.append(sum(jnp.where(named[k], gates[:, k : k + 1], 0.0) for k in range(top)))
    onehot = expert_rows(GROUP * CAP)
    choose = (dot_t(onehot, key[1]) == codes(range(GROUP))[:, None]).astype(BF)
    turned = [slice(k * tokens, (k + 1) * tokens) for k in (0, 3, 2, 1)]
    key, weight = [[jnp.concatenate([value[cut] for cut in turned]) for value in group] for group in (key, weight)]
    arrived, choose, key0, key1, weight0, weight1, *rest = tie(
        arrived, choose, *key, *weight, *near, *cuts0, *cuts1
    )
    near, cuts0, cuts1 = rest[:3], rest[3:6], rest[6:]

    chosen = dot(choose, jnp.concatenate([second_rows, *near], axis=0)).astype(BF)
    chosen = exchange(chosen.reshape(EXPERTS, GROUP * CAP, width))

    ahead, back = shift(arrived, 1), shift(arrived, -1)
    weights = (gate_weight, up_weight)
    piece = hidden_of(y, [arrived], *weights, 0)
    middle = EXPERTS * CAP // 2
    ahead, back, piece, *rest = tie(ahead, back, piece, *cuts0, *cuts1)
    cuts0, cuts1 = rest[:3], rest[3:]
    far = [shift(ahead[:middle], 1), shift(back[middle:], -1)]
    both = hidden_of(y, [ahead, back], *weights, 0)
    far0, far1, both, *rest = tie(*far, both, *cuts0, *cuts1)
    cuts0, cuts1 = rest[:3], rest[3:]

    parts0 = shifts(cuts0)
    rows = np.arange(EXPERTS * CAP)
    target = np.tile((rows // CAP * GROUP * CAP + rows % CAP).astype(np.int32), GROUP)[None]
    step = np.repeat(np.asarray([0, 1, 3, 2], np.int32), EXPERTS * CAP)[None]
    far_piece = hidden_of(y, [far0, far1], *weights, 0)
    hidden = arrange(y, target + jnp.bitwise_and(index - step + GROUP, GROUP - 1) * CAP, [piece, both, far_piece])
    units = spread(hidden)
    hidden_second = hidden_of(y, [chosen.reshape(-1, width)], *weights, 1)
    hidden_second, *rest = tie(hidden_second, *units, *parts0, *cuts1)
    units, parts0, cuts1 = [hidden, *rest[:3]], rest[3:6], rest[6:]

    parts1 = shifts(cuts1)
    units_second = [hidden_second, *spread(hidden_second)]
    back0 = exchange(project(y, units, [parts0], down_weight, 0))
    out = project(y, units_second, [parts1], down_weight, 1)
    out, key0 = tie(out, key0)
    back1 = exchange(out)
    results = [
        home(y, combine(y, back0, key0, weight0), first_rows),
        home(y, combine(y, back1, key1, weight1), second_rows),
    ]
    size = lax.axis_size("pipe")
    ahead = lax.ppermute(results[0], "pipe", [(i, i + 1) for i in range(size - 1)])
    behind = lax.ppermute(results[1], "pipe", [(i + 1, i) for i in range(size - 1)])
    first = jnp.where(pipe_index == 0, results[1], ahead)
    second = jnp.where(pipe_index == last, results[0], behind)
    return jnp.stack([first, second])[None]


def solution(mesh):
    pipe = mesh.devices.shape[0]
    split = Mesh(mesh.devices.reshape(pipe, 4, 2, GROUP), ("pipe", "x", "z", "y"))
    wide = ("x", "z", "y")
    return jax.shard_map(
        local,
        mesh=split,
        in_specs=(
            P("pipe", None, wide, None),
            P("pipe", None, wide, None),
            P("pipe", None, wide, None),
            P("pipe", None, None, wide),
            P("pipe", None, None, wide),
            P("pipe", None, wide, None),
        ),
        out_specs=P("pipe", None, wide, None),
        check_vma=False,
    )
```

```python
import functools

import jax
import jax.numpy as jnp
import numpy as np
from jax import lax
from jax.experimental import pallas as pl
from jax.experimental.pallas import tpu as pltpu
from jax.sharding import Mesh, PartitionSpec as P

EXPERTS = 8
CAP = 20
GROUP = 4
PAIR = 2
LANES = 128
STRIDE = 64
BF = jnp.bfloat16
F32 = jnp.float32


def dot(a, b):
    return jnp.dot(a, b, preferred_element_type=F32)


def dot_t(a, b):
    return lax.dot_general(a, b, (((1,), (1,)), ((), ())), preferred_element_type=F32)


def tie(values, earlier):
    anywhere = pl.BlockSpec(memory_space=pl.ANY)
    corner = pl.BlockSpec((16, LANES), lambda i: (0, 0))
    return pl.pallas_call(
        lambda *refs: None,
        out_shape=[jax.ShapeDtypeStruct(value.shape, value.dtype) for value in values],
        in_specs=[anywhere] * len(values) + [corner] * len(earlier),
        out_specs=[anywhere] * len(values),
        grid=(1,),
        input_output_aliases={i: i for i in range(len(values))},
    )(*values, *earlier)


def call(kernel, out_shape, grid, in_specs, out_specs, scratch=(), moved=0):
    return pl.pallas_call(
        kernel,
        cost_estimate=pl.CostEstimate(flops=moved * 500, transcendentals=0, bytes_accessed=moved),
        out_shape=out_shape,
        grid_spec=pltpu.PrefetchScalarGridSpec(
            num_scalar_prefetch=1, grid=grid, in_specs=in_specs, out_specs=out_specs, scratch_shapes=scratch
        ),
        compiler_params=pltpu.CompilerParams(vmem_limit_bytes=48 * 1024 * 1024),
    )


def shape(*dims):
    return jax.ShapeDtypeStruct(dims, BF)


def whole(value):
    return pl.BlockSpec(value.shape, lambda *_: (0,) * len(value.shape))


def columns_of(rows, tile):
    return pl.BlockSpec((rows, tile), lambda j, y: (0, j))


def shift(value, steps):
    return lax.ppermute(value, "y", [(i, (i + steps) % GROUP) for i in range(GROUP)])


def shifts(pieces):
    return [shift(pieces[k - 1], k) for k in range(1, GROUP)]


def spread(value):
    return [shift(value, k) for k in range(1, GROUP)]


def exchange(value):
    return lax.all_to_all(value, ("x", "z"), split_axis=0, concat_axis=0, tiled=True)


def packed(ids, gates):
    high = lax.reduce_precision(gates, 8, 7)
    middle = lax.reduce_precision(gates - high, 8, 7)
    return jnp.concatenate([ids.astype(F32), high, middle, gates - high - middle], axis=-1).astype(BF)


def unpacked(columns):
    top = columns.shape[-1] // 4
    columns = [columns[:, i * top : (i + 1) * top].astype(F32) for i in range(4)]
    return columns[0].astype(jnp.int32), (columns[1] + columns[2]) + columns[3]


def keys(ids, before, place):
    named = [ids[:, k : k + 1] == jnp.arange(LANES, dtype=jnp.int32) for k in range(ids.shape[1])]
    chose = functools.reduce(jnp.logical_or, named)
    rank = dot(before, chose.astype(BF))
    return jnp.where(chose, rank + place, -1.0).astype(BF), named


def expert_rows(per_expert):
    return np.asarray(np.arange(EXPERTS * per_expert)[:, None] // per_expert == np.arange(LANES), dtype=BF)


def codes(places):
    return np.asarray([STRIDE * place + c for _ in range(EXPERTS) for place in places for c in range(CAP)], np.float32)


def unfold(y, pick, value):
    rows, half = pick.shape[1], value.shape[1]

    def kernel(y_ref, pick_ref, value_ref, out_ref):
        out_ref[...] = dot(pick_ref[0], value_ref[...]).astype(BF)

    return call(
        kernel,
        shape(rows, 2 * half),
        (2,),
        [pl.BlockSpec((1,) + pick.shape[1:], lambda h, y: (h, 0, 0)), whole(value)],
        columns_of(rows, half),
    )(y, pick, value)


def quarters(y, down, section, runs):
    depth, part = down.shape[2], down.shape[3] // GROUP // runs
    count = (GROUP - 1) * runs

    def kernel(y_ref, down_ref, *refs):
        for i in range(count):

            @pl.when(pl.program_id(0) == i)
            def _():
                refs[i][...] = down_ref[0, 0]

    def column(i, y):
        return (0, section, 0, lax.rem(y[0] + i // runs + 1, GROUP) * runs + lax.rem(i, runs))

    cuts = call(
        kernel,
        [shape(depth, part)] * count,
        (count,),
        [pl.BlockSpec((1, 1, depth, part), column)],
        [pl.BlockSpec((depth, part), lambda k, y: (0, 0))] * count,
    )(y, down)
    return [cuts[run::runs] for run in range(runs)]


def hidden_of(y, rows, gate, up, section):
    width, block = gate.shape[2:]
    total = sum(run.shape[0] for run in rows)
    tile = 1024
    steps = width // tile

    def kernel(y_ref, gate_ref, up_ref, *refs):
        *runs, out_ref, gate_sum, up_sum = refs
        step = pl.program_id(0)

        @pl.when(step == 0)
        def _():
            gate_sum[...] = jnp.zeros_like(gate_sum)
            up_sum[...] = jnp.zeros_like(up_sum)

        value = jnp.concatenate([run[...] for run in runs], axis=0) if len(runs) > 1 else runs[0][...]
        gate_sum[...] += dot(value, gate_ref[0, 0])
        up_sum[...] += dot(value, up_ref[0, 0])

        @pl.when(step == steps - 1)
        def _():
            out_ref[...] = (jax.nn.silu(gate_sum[...]) * up_sum[...]).astype(BF)

    weights = pl.BlockSpec((1, 1, tile, block), lambda j, y: (0, section, j, 0))
    return call(
        kernel,
        shape(total, block),
        (steps,),
        [weights, weights] + [columns_of(run.shape[0], tile) for run in rows],
        pl.BlockSpec((total, block), lambda j, y: (0, 0)),
        [pltpu.VMEM((total, block), F32)] * 2,
        moved=400 * 2**20,
    )(y, gate, up, *rows)


def arrange(y, target, pieces):
    block = pieces[0].shape[1]
    rows = target.shape[1]

    def kernel(y_ref, target_ref, *refs):
        stacked = jnp.concatenate([ref[...] for ref in refs[:-1]], axis=0)
        moved = lax.broadcasted_iota(jnp.int32, (rows, rows), 0) == target_ref[...]
        refs[-1][...] = dot(moved.astype(F32).astype(BF), stacked).astype(BF)

    return call(
        kernel,
        shape(rows, block),
        (1,),
        [whole(target)] + [whole(piece) for piece in pieces],
        pl.BlockSpec((rows, block), lambda j, y: (0, 0)),
    )(y, target, *pieces)


def project(y, units, parts, down, section, moved):
    rows, depth = units[0].shape
    part = sum(group[0].shape[1] for group in parts)
    tile = part // 2
    runs = len(parts)
    flat = [value for group in parts for value in group]

    def kernel(y_ref, *refs):
        *refs, out_ref, joined = refs
        step = pl.program_id(0)

        @pl.when(step == 0)
        def _():
            for k in range(GROUP):
                joined[:, k * depth : (k + 1) * depth] = refs[k][...]

        own, others = refs[GROUP], refs[GROUP + 1 :]
        for run in range(runs):

            @pl.when(step // (2 // runs) == run)
            def _():
                mine = others[run * (GROUP - 1) : (run + 1) * (GROUP - 1)]
                matrix = jnp.concatenate([own[0, 0], *(ref[...] for ref in mine)], axis=0)
                out_ref[...] = dot(joined[...], matrix).astype(BF)

    own = pl.BlockSpec((1, 1, depth, tile), lambda j, y: (0, section, 0, y[0] * 2 + j))
    others = [columns_of(depth, tile) if runs == 1 else whole(value) for value in flat]
    out = call(
        kernel,
        shape(rows, part),
        (2,),
        [whole(unit) for unit in units] + [own] + others,
        columns_of(rows, tile),
        [pltpu.VMEM((rows, GROUP * depth), BF)],
        moved=moved,
    )(y, *units, down, *flat)
    return out.reshape(EXPERTS, GROUP * CAP, part)


def combine(here, back, key, weight, others=()):
    part, tile = back.shape[2], 896
    back = back.reshape(-1, part)
    tokens = key.shape[0] // GROUP
    onehot = expert_rows(GROUP * CAP)
    code = codes(range(GROUP))[None]
    high = lax.reduce_precision(weight, 8, 7)
    weights = [high.astype(BF), (weight - high).astype(BF)]
    given = len(others)

    def kernel(here_ref, key_ref, high_ref, low_ref, onehot_ref, code_ref, back_ref, *refs):
        expand = onehot_ref[...]
        hit = dot_t(key_ref[...], expand) == code_ref[...]
        total = 0.0
        for ref in (high_ref, low_ref):
            mix = jnp.where(hit, dot_t(ref[...], expand), 0.0).astype(BF)
            total += dot(mix, back_ref[...])
        total = total.astype(BF)
        for k in range(GROUP):
            piece = total[k * tokens : (k + 1) * tokens]
            refs[given + k][...] = piece
            if given:
                first = here_ref[1] == 0

                @pl.when(first)
                def _():
                    refs[given + GROUP + k][...] = piece

                @pl.when(jnp.logical_not(first))
                def _():
                    refs[given + GROUP + k][...] = refs[k][...]

    count = GROUP + given
    return call(
        kernel,
        [shape(tokens, part)] * count,
        (part // tile,),
        [whole(value) for value in (key, *weights, onehot, code)]
        + [columns_of(back.shape[0], tile)]
        + [columns_of(tokens, tile)] * given,
        [columns_of(tokens, tile)] * count,
    )(here, key, *weights, onehot, code, back, *others)


def send(pieces, ranks, size):
    return [
        lax.ppermute(
            pieces[k],
            ("pipe", "y"),
            [(p * GROUP + i, q * GROUP + (i + k) % GROUP) for p, q in ranks for i in range(GROUP)],
        )
        for k in range(size)
    ]


def settle(here, last, rows, ahead, behind, kept):
    tokens, part = kept[0].shape
    pieces = [*ahead, *behind, *kept]

    def kernel(here_ref, rows_ref, *refs):
        *refs, out_ref = refs
        sums = [refs[i * GROUP : (i + 1) * GROUP] for i in range(3)]
        for k in range(GROUP):

            @pl.when(pl.program_id(0) == k)
            def _():
                for slot, edge in ((0, 0), (1, last)):
                    at_edge = here_ref[1] == edge
                    value = jnp.where(at_edge, sums[2][k][...].astype(F32), sums[slot][k][...].astype(F32))
                    out_ref[slot] = (rows_ref[slot].astype(F32) + value).astype(BF)

    quarter = pl.BlockSpec((2, tokens, part), lambda k, here: (0, 0, lax.rem(here[0] + GROUP - k, GROUP)))
    return call(
        kernel,
        shape(*rows.shape),
        (GROUP,),
        [quarter] + [whole(piece) for piece in pieces],
        quarter,
    )(here, rows, *pieces)


def local(activations, expert_ids, gate_values, gate_weight, up_weight, down_weight):
    tokens, width = activations.shape[2:]
    top = expert_ids.shape[3]
    half = width // 2
    index = lax.axis_index("y").astype(jnp.int32)
    y = jnp.stack([index, lax.axis_index("pipe").astype(jnp.int32)])
    last = lax.axis_size("pipe") - 1
    first_rows, second_rows = activations[0, 0], activations[0, 1]

    before = np.asarray(np.tril(np.ones((tokens, tokens)), -1), dtype=BF)
    key, _ = keys(expert_ids[0, 0], before, 0.0)
    key = jnp.concatenate([key, jnp.where(key < 0, key, key + STRIDE)], axis=0)
    choose = (dot_t(expert_rows(2 * CAP), key) == codes(range(2))[:, None]).astype(BF)
    halves = jnp.concatenate([first_rows[:, :half], first_rows[:, half:]], axis=0)
    outgoing = dot(choose, halves).astype(BF).reshape(EXPERTS, 2 * CAP, half)
    routing = [packed(expert_ids[0, s], gate_values[0, s]) for s in range(2)]
    routing = jnp.concatenate([*routing, jnp.zeros((tokens, LANES - 8 * top), BF)], axis=1)
    arrived = exchange(outgoing)

    near = spread(second_rows)
    routing = jnp.concatenate([routing, *spread(routing)], axis=0)
    order = np.arange(EXPERTS * CAP)
    source = order // CAP * 2 * CAP + order % CAP + np.arange(2)[:, None] * CAP
    pick = np.asarray(source[:, :, None] == np.arange(EXPERTS * 2 * CAP), dtype=BF)
    arrived = unfold(y, pick, arrived.reshape(EXPERTS * 2 * CAP, half))
    (cuts0,), (cuts1,) = [quarters(y, down_weight, s, 1) for s in range(2)]

    owner = jnp.bitwise_and(index - np.arange(GROUP * tokens, dtype=np.int32)[:, None] // tokens, GROUP - 1)
    before = np.asarray(np.kron(np.eye(GROUP), np.tril(np.ones((tokens, tokens)), -1)), dtype=BF)
    key, weight = [], []
    for s in range(2):
        ids, gates = unpacked(routing[:, 4 * top * s : 4 * top * (s + 1)])
        found, named = keys(ids, before, (owner * STRIDE).astype(F32))
        key.append(found)
        weight.append(sum(jnp.where(named[k], gates[:, k : k + 1], 0.0) for k in range(top)))
    onehot = expert_rows(GROUP * CAP)
    choose = (dot_t(onehot, key[1]) == codes(range(GROUP))[:, None]).astype(BF)
    turned = [slice(k * tokens, (k + 1) * tokens) for k in (0, 3, 2, 1)]
    key, weight = [[jnp.concatenate([value[cut] for cut in turned]) for value in group] for group in (key, weight)]
    choose, key0, key1, weight0, weight1 = tie([choose, *key, *weight], [arrived, *near])

    chosen = dot(choose, jnp.concatenate([second_rows, *near], axis=0)).astype(BF)
    chosen = exchange(chosen.reshape(EXPERTS, GROUP * CAP, width))

    ahead, back = shift(arrived, 1), shift(arrived, -1)
    weights = (gate_weight, up_weight)
    middle = EXPERTS * CAP // 2
    far = [shift(ahead[:middle], 1), shift(back[middle:], -1)]
    both = hidden_of(y, [arrived, ahead, back], *weights, 0)
    up_one, down_one = [(p, p + 1) for p in range(last)], [(p + 1, p) for p in range(last)]
    before_rows = lax.ppermute(first_rows, "pipe", up_one)
    after_rows = lax.ppermute(second_rows, "pipe", down_one)
    rows = jnp.stack(
        [jnp.where(y[1] == 0, second_rows, before_rows), jnp.where(y[1] == last, first_rows, after_rows)]
    )
    rest = tie([*cuts0, *cuts1, rows], [*far, both])
    cuts0, cuts1, own_rows = rest[:3], rest[3:6], rest[6]

    parts0 = shifts(cuts0)
    rows = np.arange(EXPERTS * CAP)
    target = np.tile((rows // CAP * GROUP * CAP + rows % CAP).astype(np.int32), GROUP)[None]
    step = np.repeat(np.asarray([0, 1, 3, 2], np.int32), EXPERTS * CAP)[None]
    far_piece = hidden_of(y, far, *weights, 0)
    hidden = arrange(y, target + jnp.bitwise_and(index - step + GROUP, GROUP - 1) * CAP, [both, far_piece])
    units = spread(hidden)
    cuts1 = tie(cuts1, [*units, *parts0])
    units = [hidden, *units]

    parts1 = shifts(cuts1)
    hidden_second = hidden_of(y, [chosen.reshape(-1, width)], *weights, 1)
    out = project(y, units, [parts0], down_weight, 0, 0)
    (later,) = tie([hidden_second], [out.reshape(-1, out.shape[2])])
    units_second = [hidden_second, shift(hidden_second, 1), shift(later, 2), shift(hidden_second, 3)]
    back0 = exchange(out)
    out = project(y, units_second, [parts1], down_weight, 1, 400 * 2**20)
    out, key0 = tie([out, key0], [])
    back1 = exchange(out)
    sums0 = combine(y, back0, key0, weight0)
    ahead = send(sums0, up_one, GROUP)
    sums1 = combine(y, back1, key1, weight1, sums0)
    sums1, kept = sums1[:GROUP], sums1[GROUP:]
    behind = send(sums1, down_one, GROUP)
    kept = [kept[0], *send(kept, [(0, 0), (last, last)], GROUP)[1:]]
    return settle(y, last, own_rows, ahead, behind, kept)[None]


def solution(mesh):
    pipe = mesh.devices.shape[0]
    split = Mesh(mesh.devices.reshape(pipe, 4, 2, GROUP), ("pipe", "x", "z", "y"))
    wide = ("x", "z", "y")
    return jax.shard_map(
        local,
        mesh=split,
        in_specs=(
            P("pipe", None, wide, None),
            P("pipe", None, wide, None),
            P("pipe", None, wide, None),
            P("pipe", None, None, wide),
            P("pipe", None, None, wide),
            P("pipe", None, wide, None),
        ),
        out_specs=P("pipe", None, wide, None),
        check_vma=False,
    )
```

```python
import functools

import jax
import jax.numpy as jnp
import numpy as np
from jax import lax
from jax.experimental import pallas as pl
from jax.experimental.pallas import tpu as pltpu
from jax.sharding import Mesh, PartitionSpec as P

EXPERTS = 8
CAP = 20
GROUP = 4
PAIR = 2
LANES = 128
STRIDE = 64
BF = jnp.bfloat16
F32 = jnp.float32


def dot(a, b):
    return jnp.dot(a, b, preferred_element_type=F32)


def dot_t(a, b):
    return lax.dot_general(a, b, (((1,), (1,)), ((), ())), preferred_element_type=F32)


def tie(values, earlier):
    anywhere = pl.BlockSpec(memory_space=pl.ANY)
    corner = pl.BlockSpec((16, LANES), lambda i: (0, 0))
    return pl.pallas_call(
        lambda *refs: None,
        out_shape=[jax.ShapeDtypeStruct(value.shape, value.dtype) for value in values],
        in_specs=[anywhere] * len(values) + [corner] * len(earlier),
        out_specs=[anywhere] * len(values),
        grid=(1,),
        input_output_aliases={i: i for i in range(len(values))},
    )(*values, *earlier)


def call(kernel, out_shape, grid, in_specs, out_specs, scratch=(), moved=0):
    return pl.pallas_call(
        kernel,
        cost_estimate=pl.CostEstimate(flops=moved * 500, transcendentals=0, bytes_accessed=moved),
        out_shape=out_shape,
        grid_spec=pltpu.PrefetchScalarGridSpec(
            num_scalar_prefetch=1, grid=grid, in_specs=in_specs, out_specs=out_specs, scratch_shapes=scratch
        ),
        compiler_params=pltpu.CompilerParams(vmem_limit_bytes=48 * 1024 * 1024),
    )


def shape(*dims):
    return jax.ShapeDtypeStruct(dims, BF)


def whole(value):
    return pl.BlockSpec(value.shape, lambda *_: (0,) * len(value.shape))


def columns_of(rows, tile):
    return pl.BlockSpec((rows, tile), lambda j, y: (0, j))


def shift(value, steps):
    return lax.ppermute(value, "y", [(i, (i + steps) % GROUP) for i in range(GROUP)])


def shifts(pieces):
    return [shift(pieces[k - 1], k) for k in range(1, GROUP)]


def spread(value):
    return [shift(value, k) for k in range(1, GROUP)]


def exchange(value):
    return lax.all_to_all(value, ("x", "z"), split_axis=0, concat_axis=0, tiled=True)


def packed(ids, gates):
    high = lax.reduce_precision(gates, 8, 7)
    middle = lax.reduce_precision(gates - high, 8, 7)
    return jnp.concatenate([ids.astype(F32), high, middle, gates - high - middle], axis=-1).astype(BF)


def unpacked(columns):
    top = columns.shape[-1] // 4
    columns = [columns[:, i * top : (i + 1) * top].astype(F32) for i in range(4)]
    return columns[0].astype(jnp.int32), (columns[1] + columns[2]) + columns[3]


def keys(ids, before, place):
    named = [ids[:, k : k + 1] == jnp.arange(LANES, dtype=jnp.int32) for k in range(ids.shape[1])]
    chose = functools.reduce(jnp.logical_or, named)
    rank = dot(before, chose.astype(BF))
    return jnp.where(chose, rank + place, -1.0).astype(BF), named


def expert_rows(per_expert):
    return np.asarray(np.arange(EXPERTS * per_expert)[:, None] // per_expert == np.arange(LANES), dtype=BF)


def codes(places):
    return np.asarray([STRIDE * place + c for _ in range(EXPERTS) for place in places for c in range(CAP)], np.float32)


def unfold(y, pick, value):
    rows, half = pick.shape[1] // 2, value.shape[1]

    def kernel(y_ref, pick_ref, value_ref, *refs):
        joined = dot(pick_ref[0], value_ref[...]).astype(BF)
        for i in range(2):
            refs[i][...] = joined[i * rows : (i + 1) * rows]

    return call(
        kernel,
        [shape(rows, 2 * half)] * 2,
        (2,),
        [pl.BlockSpec((1,) + pick.shape[1:], lambda h, y: (h, 0, 0)), whole(value)],
        [columns_of(rows, half)] * 2,
    )(y, pick, value)


def quarters(y, down, section, runs):
    depth, part = down.shape[2], down.shape[3] // GROUP // runs
    count = (GROUP - 1) * runs

    def kernel(y_ref, down_ref, *refs):
        for i in range(count):

            @pl.when(pl.program_id(0) == i)
            def _():
                refs[i][...] = down_ref[0, 0]

    def column(i, y):
        return (0, section, 0, lax.rem(y[0] + i // runs + 1, GROUP) * runs + lax.rem(i, runs))

    cuts = call(
        kernel,
        [shape(depth, part)] * count,
        (count,),
        [pl.BlockSpec((1, 1, depth, part), column)],
        [pl.BlockSpec((depth, part), lambda k, y: (0, 0))] * count,
    )(y, down)
    return [cuts[run::runs] for run in range(runs)]


def hidden_of(y, rows, gate, up, section):
    width, block = gate.shape[2:]
    total = sum(run.shape[0] for run in rows)
    tile = 1024
    steps = width // tile

    def kernel(y_ref, gate_ref, up_ref, *refs):
        *runs, out_ref, gate_sum, up_sum = refs
        step = pl.program_id(0)

        @pl.when(step == 0)
        def _():
            gate_sum[...] = jnp.zeros_like(gate_sum)
            up_sum[...] = jnp.zeros_like(up_sum)

        value = jnp.concatenate([run[...] for run in runs], axis=0) if len(runs) > 1 else runs[0][...]
        gate_sum[...] += dot(value, gate_ref[0, 0])
        up_sum[...] += dot(value, up_ref[0, 0])

        @pl.when(step == steps - 1)
        def _():
            out_ref[...] = (jax.nn.silu(gate_sum[...]) * up_sum[...]).astype(BF)

    weights = pl.BlockSpec((1, 1, tile, block), lambda j, y: (0, section, j, 0))
    return call(
        kernel,
        shape(total, block),
        (steps,),
        [weights, weights] + [columns_of(run.shape[0], tile) for run in rows],
        pl.BlockSpec((total, block), lambda j, y: (0, 0)),
        [pltpu.VMEM((total, block), F32)] * 2,
        moved=400 * 2**20,
    )(y, gate, up, *rows)


def arrange(y, target, pieces):
    block = pieces[0].shape[1]
    rows = target.shape[1]

    def kernel(y_ref, target_ref, *refs):
        stacked = jnp.concatenate([ref[...] for ref in refs[:-1]], axis=0)
        moved = lax.broadcasted_iota(jnp.int32, (rows, rows), 0) == target_ref[...]
        refs[-1][...] = dot(moved.astype(F32).astype(BF), stacked).astype(BF)

    return call(
        kernel,
        shape(rows, block),
        (1,),
        [whole(target)] + [whole(piece) for piece in pieces],
        pl.BlockSpec((rows, block), lambda j, y: (0, 0)),
    )(y, target, *pieces)


def project(y, units, parts, down, section, moved):
    rows, depth = units[0].shape
    part = sum(group[0].shape[1] for group in parts)
    tile = part // 2
    runs = len(parts)
    flat = [value for group in parts for value in group]

    def kernel(y_ref, *refs):
        *refs, out_ref, joined = refs
        step = pl.program_id(0)

        @pl.when(step == 0)
        def _():
            for k in range(GROUP):
                joined[:, k * depth : (k + 1) * depth] = refs[k][...]

        own, others = refs[GROUP], refs[GROUP + 1 :]
        for run in range(runs):

            @pl.when(step // (2 // runs) == run)
            def _():
                mine = others[run * (GROUP - 1) : (run + 1) * (GROUP - 1)]
                matrix = jnp.concatenate([own[0, 0], *(ref[...] for ref in mine)], axis=0)
                out_ref[...] = dot(joined[...], matrix).astype(BF)

    own = pl.BlockSpec((1, 1, depth, tile), lambda j, y: (0, section, 0, y[0] * 2 + j))
    others = [columns_of(depth, tile) if runs == 1 else whole(value) for value in flat]
    out = call(
        kernel,
        shape(rows, part),
        (2,),
        [whole(unit) for unit in units] + [own] + others,
        columns_of(rows, tile),
        [pltpu.VMEM((rows, GROUP * depth), BF)],
        moved=moved,
    )(y, *units, down, *flat)
    return out.reshape(EXPERTS, GROUP * CAP, part)


def combine(here, back, key, weight, rows=()):
    part, tile = back.shape[2], 896
    back = back.reshape(-1, part)
    tokens = key.shape[0] // GROUP
    onehot = expert_rows(GROUP * CAP)
    code = codes(range(GROUP))[None]
    high = lax.reduce_precision(weight, 8, 7)
    weights = [high.astype(BF), (weight - high).astype(BF)]
    given = len(rows)

    def kernel(here_ref, key_ref, high_ref, low_ref, onehot_ref, code_ref, back_ref, *refs):
        expand = onehot_ref[...]
        hit = dot_t(key_ref[...], expand) == code_ref[...]
        total = 0.0
        for ref in (high_ref, low_ref):
            mix = jnp.where(hit, dot_t(ref[...], expand), 0.0).astype(BF)
            total += dot(mix, back_ref[...])
        for k in range(GROUP):
            piece = total[k * tokens : (k + 1) * tokens]
            if given:
                piece = piece + refs[k][...].astype(F32)
            refs[given + k][...] = piece.astype(BF)

    own = pl.BlockSpec((tokens, tile), lambda j, here: (0, here[0] * (part // tile) + j))
    return call(
        kernel,
        [shape(tokens, part)] * GROUP,
        (part // tile,),
        [whole(value) for value in (key, *weights, onehot, code)] + [columns_of(back.shape[0], tile)] + [own] * given,
        [columns_of(tokens, tile)] * GROUP,
    )(here, key, *weights, onehot, code, back, *rows)


def home(here, totals, rows):
    pieces = [totals[0], *shifts(totals[1:])]
    tokens, part = totals[0].shape

    def kernel(here_ref, rows_ref, *refs):
        for k in range(GROUP):

            @pl.when(pl.program_id(0) == k)
            def _():
                refs[-1][...] = (rows_ref[...].astype(F32) + refs[k][...].astype(F32)).astype(BF)

    quarter = pl.BlockSpec((tokens, part), lambda k, here: (0, lax.rem(here[0] + GROUP - k, GROUP)))
    return call(
        kernel,
        shape(*rows.shape),
        (GROUP,),
        [quarter] + [whole(piece) for piece in pieces],
        quarter,
    )(here, rows, *pieces)


def send(pieces, ranks, size):
    return [
        lax.ppermute(
            pieces[k],
            ("pipe", "y"),
            [(p * GROUP + i, q * GROUP + (i + k) % GROUP) for p, q in ranks for i in range(GROUP)],
        )
        for k in range(size)
    ]


def settle(here, last, ahead, own, behind, kept):
    tokens, part = kept[0].shape

    def kernel(here_ref, ahead_ref, own_ref, *refs):
        *refs, out_ref = refs
        for k in range(GROUP):

            @pl.when(pl.program_id(0) == k)
            def _():
                first, final = here_ref[1] == 0, here_ref[1] == last
                out_ref[0] = jnp.where(first, refs[GROUP + k][...], ahead_ref[...])
                out_ref[1] = jnp.where(final, own_ref[...], refs[k][...])

    def column(k, here):
        return lax.rem(here[0] + GROUP - k, GROUP)

    quarter = pl.BlockSpec((tokens, part), lambda k, here: (0, column(k, here)))
    return call(
        kernel,
        shape(2, *own.shape),
        (GROUP,),
        [quarter] * 2 + [whole(piece) for piece in (*behind, *kept)],
        pl.BlockSpec((2, tokens, part), lambda k, here: (0, 0, column(k, here))),
    )(here, ahead, own, *behind, *kept)


def local(activations, expert_ids, gate_values, gate_weight, up_weight, down_weight):
    tokens, width = activations.shape[2:]
    top = expert_ids.shape[3]
    half = width // 2
    index = lax.axis_index("y").astype(jnp.int32)
    y = jnp.stack([index, lax.axis_index("pipe").astype(jnp.int32)])
    last = lax.axis_size("pipe") - 1
    first_rows, second_rows = activations[0, 0], activations[0, 1]

    before = np.asarray(np.tril(np.ones((tokens, tokens)), -1), dtype=BF)
    key, _ = keys(expert_ids[0, 0], before, 0.0)
    key = jnp.concatenate([key, jnp.where(key < 0, key, key + STRIDE)], axis=0)
    choose = (dot_t(expert_rows(2 * CAP), key) == codes(range(2))[:, None]).astype(BF)
    halves = jnp.concatenate([first_rows[:, :half], first_rows[:, half:]], axis=0)
    outgoing = dot(choose, halves).astype(BF).reshape(EXPERTS, 2 * CAP, half)
    routing = [packed(expert_ids[0, s], gate_values[0, s]) for s in range(2)]
    routing = jnp.concatenate([*routing, jnp.zeros((tokens, LANES - 8 * top), BF)], axis=1)
    arrived = exchange(outgoing)

    near = spread(second_rows)
    routing = jnp.concatenate([routing, *spread(routing)], axis=0)
    order = np.arange(EXPERTS * CAP)
    source = order // CAP * 2 * CAP + order % CAP + np.arange(2)[:, None] * CAP
    pick = np.asarray(source[:, :, None] == np.arange(EXPERTS * 2 * CAP), dtype=BF)
    arrived = unfold(y, pick, arrived.reshape(EXPERTS * 2 * CAP, half))
    (cuts0,), (cuts1,) = [quarters(y, down_weight, s, 1) for s in range(2)]

    owner = jnp.bitwise_and(index - np.arange(GROUP * tokens, dtype=np.int32)[:, None] // tokens, GROUP - 1)
    before = np.asarray(np.kron(np.eye(GROUP), np.tril(np.ones((tokens, tokens)), -1)), dtype=BF)
    key, weight = [], []
    for s in range(2):
        ids, gates = unpacked(routing[:, 4 * top * s : 4 * top * (s + 1)])
        found, named = keys(ids, before, (owner * STRIDE).astype(F32))
        key.append(found)
        weight.append(sum(jnp.where(named[k], gates[:, k : k + 1], 0.0) for k in range(top)))
    onehot = expert_rows(GROUP * CAP)
    choose = (dot_t(onehot, key[1]) == codes(range(GROUP))[:, None]).astype(BF)
    turned = [slice(k * tokens, (k + 1) * tokens) for k in (0, 3, 2, 1)]
    key, weight = [[jnp.concatenate([value[cut] for cut in turned]) for value in group] for group in (key, weight)]
    choose, key0, key1, weight0, weight1 = tie([choose, *key, *weight], [*arrived, *near])

    chosen = dot(choose, jnp.concatenate([second_rows, *near], axis=0)).astype(BF)
    chosen = exchange(chosen.reshape(EXPERTS, GROUP * CAP, width))

    ahead, back = [[shift(run, steps) for run in arrived] for steps in (1, -1)]
    weights = (gate_weight, up_weight)
    far = [shift(ahead[0], 1), shift(back[1], -1)]
    both = hidden_of(y, [*arrived, *ahead, *back], *weights, 0)
    up_one, down_one = [(p, p + 1) for p in range(last)], [(p + 1, p) for p in range(last)]
    rest = tie([*cuts0, *cuts1], [*far, both])
    cuts0, cuts1 = rest[:3], rest[3:]

    parts0 = shifts(cuts0)
    rows = np.arange(EXPERTS * CAP)
    target = np.tile((rows // CAP * GROUP * CAP + rows % CAP).astype(np.int32), GROUP)[None]
    step = np.repeat(np.asarray([0, 1, 3, 2], np.int32), EXPERTS * CAP)[None]
    far_piece = hidden_of(y, far, *weights, 0)
    hidden = arrange(y, target + jnp.bitwise_and(index - step + GROUP, GROUP - 1) * CAP, [both, far_piece])
    units = spread(hidden)
    cuts1 = tie(cuts1, [*units, *parts0])
    units = [hidden, *units]

    parts1 = shifts(cuts1)
    out = project(y, units, [parts0], down_weight, 0, 0)
    (here,) = tie([y], [out.reshape(-1, out.shape[2])])
    hidden_second = hidden_of(here, [chosen.reshape(-1, width)], *weights, 1)
    units_second = [hidden_second, *spread(hidden_second)]
    back0 = exchange(out)
    out = project(y, units_second, [parts1], down_weight, 1, 0)
    out, key0 = tie([out, key0], [])
    back1 = exchange(out)
    result0 = home(y, combine(y, back0, key0, weight0), first_rows)
    ahead = lax.ppermute(result0, "pipe", up_one)
    turned = [second_rows, near[2], near[1], near[0]]
    sums1 = combine(y, back1, key1, weight1, turned)
    behind = send(sums1, down_one, GROUP)
    kept = [sums1[0], *send(sums1, [(0, 0)], GROUP)[1:]]
    return settle(y, last, ahead, result0, behind, kept)[None]


def solution(mesh):
    pipe = mesh.devices.shape[0]
    split = Mesh(mesh.devices.reshape(pipe, 4, 2, GROUP), ("pipe", "x", "z", "y"))
    wide = ("x", "z", "y")
    return jax.shard_map(
        local,
        mesh=split,
        in_specs=(
            P("pipe", None, wide, None),
            P("pipe", None, wide, None),
            P("pipe", None, wide, None),
            P("pipe", None, None, wide),
            P("pipe", None, None, wide),
            P("pipe", None, wide, None),
        ),
        out_specs=P("pipe", None, wide, None),
        check_vma=False,
    )
```

```python
import functools

import jax
import jax.numpy as jnp
import numpy as np
from jax import lax
from jax.experimental import pallas as pl
from jax.experimental.pallas import tpu as pltpu
from jax.sharding import Mesh, PartitionSpec as P

EXPERTS = 8
CAP = 20
GROUP = 4
PAIR = 2
LANES = 128
STRIDE = 64
BF = jnp.bfloat16
F32 = jnp.float32


def dot(a, b):
    return jnp.dot(a, b, preferred_element_type=F32)


def dot_t(a, b):
    return lax.dot_general(a, b, (((1,), (1,)), ((), ())), preferred_element_type=F32)


def tie(values, earlier):
    anywhere = pl.BlockSpec(memory_space=pl.ANY)
    corner = pl.BlockSpec((16, LANES), lambda i: (0, 0))
    return pl.pallas_call(
        lambda *refs: None,
        out_shape=[jax.ShapeDtypeStruct(value.shape, value.dtype) for value in values],
        in_specs=[anywhere] * len(values) + [corner] * len(earlier),
        out_specs=[anywhere] * len(values),
        grid=(1,),
        input_output_aliases={i: i for i in range(len(values))},
    )(*values, *earlier)


def call(kernel, out_shape, grid, in_specs, out_specs, scratch=(), moved=0):
    return pl.pallas_call(
        kernel,
        cost_estimate=pl.CostEstimate(flops=moved * 500, transcendentals=0, bytes_accessed=moved),
        out_shape=out_shape,
        grid_spec=pltpu.PrefetchScalarGridSpec(
            num_scalar_prefetch=1, grid=grid, in_specs=in_specs, out_specs=out_specs, scratch_shapes=scratch
        ),
        compiler_params=pltpu.CompilerParams(vmem_limit_bytes=48 * 1024 * 1024),
    )


def shape(*dims):
    return jax.ShapeDtypeStruct(dims, BF)


def whole(value):
    return pl.BlockSpec(value.shape, lambda *_: (0,) * len(value.shape))


def columns_of(rows, tile):
    return pl.BlockSpec((rows, tile), lambda j, y: (0, j))


def shift(value, steps):
    return lax.ppermute(value, "y", [(i, (i + steps) % GROUP) for i in range(GROUP)])


def shifts(pieces):
    return [shift(pieces[k - 1], k) for k in range(1, GROUP)]


def spread(value):
    return [shift(value, k) for k in range(1, GROUP)]


def exchange(value):
    return lax.all_to_all(value, ("x", "z"), split_axis=0, concat_axis=0, tiled=True)


def packed(ids, gates):
    high = lax.reduce_precision(gates, 8, 7)
    middle = lax.reduce_precision(gates - high, 8, 7)
    return jnp.concatenate([ids.astype(F32), high, middle, gates - high - middle], axis=-1).astype(BF)


def unpacked(columns):
    top = columns.shape[-1] // 4
    columns = [columns[:, i * top : (i + 1) * top].astype(F32) for i in range(4)]
    return columns[0].astype(jnp.int32), (columns[1] + columns[2]) + columns[3]


def keys(ids, before, place):
    named = [ids[:, k : k + 1] == jnp.arange(LANES, dtype=jnp.int32) for k in range(ids.shape[1])]
    chose = functools.reduce(jnp.logical_or, named)
    rank = dot(before, chose.astype(BF))
    return jnp.where(chose, rank + place, -1.0).astype(BF), named


def expert_rows(per_expert):
    return np.asarray(np.arange(EXPERTS * per_expert)[:, None] // per_expert == np.arange(LANES), dtype=BF)


def codes(places):
    return np.asarray([STRIDE * place + c for _ in range(EXPERTS) for place in places for c in range(CAP)], np.float32)


def unfold(y, pick, value):
    rows, half = pick.shape[1] // 2, value.shape[1]

    def kernel(y_ref, pick_ref, value_ref, *refs):
        joined = dot(pick_ref[0], value_ref[...]).astype(BF)
        for i in range(2):
            refs[i][...] = joined[i * rows : (i + 1) * rows]

    return call(
        kernel,
        [shape(rows, 2 * half)] * 2,
        (2,),
        [pl.BlockSpec((1,) + pick.shape[1:], lambda h, y: (h, 0, 0)), whole(value)],
        [columns_of(rows, half)] * 2,
    )(y, pick, value)


def quarters(y, down, section, runs):
    depth, part = down.shape[2], down.shape[3] // GROUP // runs
    count = (GROUP - 1) * runs

    def kernel(y_ref, down_ref, *refs):
        for i in range(count):

            @pl.when(pl.program_id(0) == i)
            def _():
                refs[i][...] = down_ref[0, 0]

    def column(i, y):
        return (0, section, 0, lax.rem(y[0] + i // runs + 1, GROUP) * runs + lax.rem(i, runs))

    cuts = call(
        kernel,
        [shape(depth, part)] * count,
        (count,),
        [pl.BlockSpec((1, 1, depth, part), column)],
        [pl.BlockSpec((depth, part), lambda k, y: (0, 0))] * count,
    )(y, down)
    return [cuts[run::runs] for run in range(runs)]


def hidden_of(y, rows, gate, up, section):
    width, block = gate.shape[2:]
    total = sum(run.shape[0] for run in rows)
    tile = 1024
    steps = width // tile

    def kernel(y_ref, gate_ref, up_ref, *refs):
        *runs, out_ref, gate_sum, up_sum = refs
        step = pl.program_id(0)

        @pl.when(step == 0)
        def _():
            gate_sum[...] = jnp.zeros_like(gate_sum)
            up_sum[...] = jnp.zeros_like(up_sum)

        value = jnp.concatenate([run[...] for run in runs], axis=0) if len(runs) > 1 else runs[0][...]
        gate_sum[...] += dot(value, gate_ref[0, 0])
        up_sum[...] += dot(value, up_ref[0, 0])

        @pl.when(step == steps - 1)
        def _():
            out_ref[...] = (jax.nn.silu(gate_sum[...]) * up_sum[...]).astype(BF)

    weights = pl.BlockSpec((1, 1, tile, block), lambda j, y: (0, section, j, 0))
    return call(
        kernel,
        shape(total, block),
        (steps,),
        [weights, weights] + [columns_of(run.shape[0], tile) for run in rows],
        pl.BlockSpec((total, block), lambda j, y: (0, 0)),
        [pltpu.VMEM((total, block), F32)] * 2,
        moved=400 * 2**20,
    )(y, gate, up, *rows)


def arrange(y, target, pieces):
    block = pieces[0].shape[1]
    rows = target.shape[1]

    def kernel(y_ref, target_ref, *refs):
        stacked = jnp.concatenate([ref[...] for ref in refs[:-1]], axis=0)
        moved = lax.broadcasted_iota(jnp.int32, (rows, rows), 0) == target_ref[...]
        refs[-1][...] = dot(moved.astype(F32).astype(BF), stacked).astype(BF)

    return call(
        kernel,
        shape(rows, block),
        (1,),
        [whole(target)] + [whole(piece) for piece in pieces],
        pl.BlockSpec((rows, block), lambda j, y: (0, 0)),
    )(y, target, *pieces)


def project(y, units, parts, down, section, moved):
    rows, depth = units[0].shape
    part = sum(group[0].shape[1] for group in parts)
    tile = part // 2
    runs = len(parts)
    flat = [value for group in parts for value in group]

    def kernel(y_ref, *refs):
        *refs, out_ref, joined = refs
        step = pl.program_id(0)

        @pl.when(step == 0)
        def _():
            for k in range(GROUP):
                joined[:, k * depth : (k + 1) * depth] = refs[k][...]

        own, others = refs[GROUP], refs[GROUP + 1 :]
        for run in range(runs):

            @pl.when(step // (2 // runs) == run)
            def _():
                mine = others[run * (GROUP - 1) : (run + 1) * (GROUP - 1)]
                matrix = jnp.concatenate([own[0, 0], *(ref[...] for ref in mine)], axis=0)
                out_ref[...] = dot(joined[...], matrix).astype(BF)

    own = pl.BlockSpec((1, 1, depth, tile), lambda j, y: (0, section, 0, y[0] * 2 + j))
    others = [columns_of(depth, tile) if runs == 1 else whole(value) for value in flat]
    out = call(
        kernel,
        shape(rows, part),
        (2,),
        [whole(unit) for unit in units] + [own] + others,
        columns_of(rows, tile),
        [pltpu.VMEM((rows, GROUP * depth), BF)],
        moved=moved,
    )(y, *units, down, *flat)
    return out.reshape(EXPERTS, GROUP * CAP, part)


def combine(here, back, key, weight, rows=()):
    part, tile = back.shape[2], 896
    back = back.reshape(-1, part)
    tokens = key.shape[0] // GROUP
    onehot = expert_rows(GROUP * CAP)
    code = codes(range(GROUP))[None]
    high = lax.reduce_precision(weight, 8, 7)
    weights = [high.astype(BF), (weight - high).astype(BF)]
    given = len(rows)

    def kernel(here_ref, key_ref, high_ref, low_ref, onehot_ref, code_ref, back_ref, *refs):
        expand = onehot_ref[...]
        hit = dot_t(key_ref[...], expand) == code_ref[...]
        total = 0.0
        for ref in (high_ref, low_ref):
            mix = jnp.where(hit, dot_t(ref[...], expand), 0.0).astype(BF)
            total += dot(mix, back_ref[...])
        for k in range(GROUP):
            piece = total[k * tokens : (k + 1) * tokens]
            if given:
                piece = piece + refs[k][...].astype(F32)
            refs[given + k][...] = piece.astype(BF)

    own = pl.BlockSpec((tokens, tile), lambda j, here: (0, here[0] * (part // tile) + j))
    return call(
        kernel,
        [shape(tokens, part)] * GROUP,
        (part // tile,),
        [whole(value) for value in (key, *weights, onehot, code)] + [columns_of(back.shape[0], tile)] + [own] * given,
        [columns_of(tokens, tile)] * GROUP,
    )(here, key, *weights, onehot, code, back, *rows)


def home(here, totals, rows):
    pieces = [totals[0], *shifts(totals[1:])]
    tokens, part = totals[0].shape

    def kernel(here_ref, rows_ref, *refs):
        for k in range(GROUP):

            @pl.when(pl.program_id(0) == k)
            def _():
                refs[-1][...] = (rows_ref[...].astype(F32) + refs[k][...].astype(F32)).astype(BF)

    quarter = pl.BlockSpec((tokens, part), lambda k, here: (0, lax.rem(here[0] + GROUP - k, GROUP)))
    return call(
        kernel,
        shape(*rows.shape),
        (GROUP,),
        [quarter] + [whole(piece) for piece in pieces],
        quarter,
    )(here, rows, *pieces)


def send(pieces, ranks, size):
    return [
        lax.ppermute(
            pieces[k],
            ("pipe", "y"),
            [(p * GROUP + i, q * GROUP + (i + k) % GROUP) for p, q in ranks for i in range(GROUP)],
        )
        for k in range(size)
    ]


def settle(here, last, ahead, own, behind, kept):
    tokens, part = kept[0].shape

    def kernel(here_ref, ahead_ref, own_ref, *refs):
        *refs, out_ref = refs
        for k in range(GROUP):

            @pl.when(pl.program_id(0) == k)
            def _():
                first, final = here_ref[1] == 0, here_ref[1] == last
                out_ref[0] = jnp.where(first, refs[GROUP + k][...], ahead_ref[...])
                out_ref[1] = jnp.where(final, own_ref[...], refs[k][...])

    def column(k, here):
        return lax.rem(here[0] + GROUP - k, GROUP)

    quarter = pl.BlockSpec((tokens, part), lambda k, here: (0, column(k, here)))
    return call(
        kernel,
        shape(2, *own.shape),
        (GROUP,),
        [quarter] * 2 + [whole(piece) for piece in (*behind, *kept)],
        pl.BlockSpec((2, tokens, part), lambda k, here: (0, 0, column(k, here))),
    )(here, ahead, own, *behind, *kept)


def local(activations, expert_ids, gate_values, gate_weight, up_weight, down_weight):
    tokens, width = activations.shape[2:]
    top = expert_ids.shape[3]
    half = width // 2
    index = lax.axis_index("y").astype(jnp.int32)
    y = jnp.stack([index, lax.axis_index("pipe").astype(jnp.int32)])
    last = lax.axis_size("pipe") - 1
    first_rows, second_rows = activations[0, 0], activations[0, 1]

    before = np.asarray(np.tril(np.ones((tokens, tokens)), -1), dtype=BF)
    key, _ = keys(expert_ids[0, 0], before, 0.0)
    key = jnp.concatenate([key, jnp.where(key < 0, key, key + STRIDE)], axis=0)
    choose = (dot_t(expert_rows(2 * CAP), key) == codes(range(2))[:, None]).astype(BF)
    halves = jnp.concatenate([first_rows[:, :half], first_rows[:, half:]], axis=0)
    outgoing = dot(choose, halves).astype(BF).reshape(EXPERTS, 2 * CAP, half)
    routing = [packed(expert_ids[0, s], gate_values[0, s]) for s in range(2)]
    routing = jnp.concatenate([*routing, jnp.zeros((tokens, LANES - 8 * top), BF)], axis=1)
    arrived = exchange(outgoing)

    near = spread(second_rows)
    routing = jnp.concatenate([routing, *spread(routing)], axis=0)
    order = np.arange(EXPERTS * CAP)
    source = order // CAP * 2 * CAP + order % CAP + np.arange(2)[:, None] * CAP
    pick = np.asarray(source[:, :, None] == np.arange(EXPERTS * 2 * CAP), dtype=BF)
    arrived = unfold(y, pick, arrived.reshape(EXPERTS * 2 * CAP, half))
    (cuts0,), (cuts1,) = [quarters(y, down_weight, s, 1) for s in range(2)]

    owner = jnp.bitwise_and(index - np.arange(GROUP * tokens, dtype=np.int32)[:, None] // tokens, GROUP - 1)
    before = np.asarray(np.kron(np.eye(GROUP), np.tril(np.ones((tokens, tokens)), -1)), dtype=BF)
    key, weight = [], []
    for s in range(2):
        ids, gates = unpacked(routing[:, 4 * top * s : 4 * top * (s + 1)])
        found, named = keys(ids, before, (owner * STRIDE).astype(F32))
        key.append(found)
        weight.append(sum(jnp.where(named[k], gates[:, k : k + 1], 0.0) for k in range(top)))
    onehot = expert_rows(GROUP * CAP)
    choose = (dot_t(onehot, key[1]) == codes(range(GROUP))[:, None]).astype(BF)
    turned = [slice(k * tokens, (k + 1) * tokens) for k in (0, 3, 2, 1)]
    key, weight = [[jnp.concatenate([value[cut] for cut in turned]) for value in group] for group in (key, weight)]
    choose, key0, key1, weight0, weight1 = tie([choose, *key, *weight], [*arrived, *near])

    chosen = dot(choose, jnp.concatenate([second_rows, *near], axis=0)).astype(BF)
    chosen = exchange(chosen.reshape(EXPERTS, GROUP * CAP, width))

    ahead, back = [[shift(run, steps) for run in arrived] for steps in (1, -1)]
    weights = (gate_weight, up_weight)
    far = [shift(ahead[0], 1), shift(back[1], -1)]
    both = hidden_of(y, [*arrived, *ahead, *back], *weights, 0)
    up_one, down_one = [(p, p + 1) for p in range(last)], [(p + 1, p) for p in range(last)]
    opposite = shift(cuts0[1], 2)
    cut1, cut3, *cuts1 = tie([cuts0[0], cuts0[2], *cuts1], [*far, both, opposite])

    parts0 = [shift(cut1, 1), opposite, shift(cut3, 3)]
    rows = np.arange(EXPERTS * CAP)
    target = np.tile((rows // CAP * GROUP * CAP + rows % CAP).astype(np.int32), GROUP)[None]
    step = np.repeat(np.asarray([0, 1, 3, 2], np.int32), EXPERTS * CAP)[None]
    far_piece = hidden_of(y, far, *weights, 0)
    hidden = arrange(y, target + jnp.bitwise_and(index - step + GROUP, GROUP - 1) * CAP, [both, far_piece])
    units = spread(hidden)
    cuts1 = tie(cuts1, [*units, *parts0])
    units = [hidden, *units]

    parts1 = shifts(cuts1)
    out = project(y, units, [parts0], down_weight, 0, 0)
    (here,) = tie([y], [out.reshape(-1, out.shape[2])])
    hidden_second = hidden_of(here, [chosen.reshape(-1, width)], *weights, 1)
    units_second = [hidden_second, *spread(hidden_second)]
    back0 = exchange(out)
    out = project(y, units_second, [parts1], down_weight, 1, 0)
    out, key0 = tie([out, key0], [])
    back1 = exchange(out)
    result0 = home(y, combine(y, back0, key0, weight0), first_rows)
    ahead = lax.ppermute(result0, "pipe", up_one)
    turned = [second_rows, near[2], near[1], near[0]]
    sums1 = combine(y, back1, key1, weight1, turned)
    behind = send(sums1, down_one, GROUP)
    kept = [sums1[0], *send(sums1, [(0, 0)], GROUP)[1:]]
    return settle(y, last, ahead, result0, behind, kept)[None]


def solution(mesh):
    pipe = mesh.devices.shape[0]
    split = Mesh(mesh.devices.reshape(pipe, 4, 2, GROUP), ("pipe", "x", "z", "y"))
    wide = ("x", "z", "y")
    return jax.shard_map(
        local,
        mesh=split,
        in_specs=(
            P("pipe", None, wide, None),
            P("pipe", None, wide, None),
            P("pipe", None, wide, None),
            P("pipe", None, None, wide),
            P("pipe", None, None, wide),
            P("pipe", None, wide, None),
        ),
        out_specs=P("pipe", None, wide, None),
        check_vma=False,
    )
```

```python
import functools

import jax
import jax.numpy as jnp
import numpy as np
from jax import lax
from jax.experimental import pallas as pl
from jax.experimental.pallas import tpu as pltpu
from jax.sharding import Mesh, PartitionSpec as P

EXPERTS = 8
CAP = 20
GROUP = 4
PAIR = 2
LANES = 128
STRIDE = 64
BF = jnp.bfloat16
F32 = jnp.float32


def dot(a, b):
    return jnp.dot(a, b, preferred_element_type=F32)


def dot_t(a, b):
    return lax.dot_general(a, b, (((1,), (1,)), ((), ())), preferred_element_type=F32)


def tie(values, earlier):
    anywhere = pl.BlockSpec(memory_space=pl.ANY)
    corner = pl.BlockSpec((16, LANES), lambda i: (0, 0))
    return pl.pallas_call(
        lambda *refs: None,
        out_shape=[jax.ShapeDtypeStruct(value.shape, value.dtype) for value in values],
        in_specs=[anywhere] * len(values) + [corner] * len(earlier),
        out_specs=[anywhere] * len(values),
        grid=(1,),
        input_output_aliases={i: i for i in range(len(values))},
    )(*values, *earlier)


def call(kernel, out_shape, grid, in_specs, out_specs, scratch=(), moved=0):
    return pl.pallas_call(
        kernel,
        cost_estimate=pl.CostEstimate(flops=moved * 500, transcendentals=0, bytes_accessed=moved),
        out_shape=out_shape,
        grid_spec=pltpu.PrefetchScalarGridSpec(
            num_scalar_prefetch=1, grid=grid, in_specs=in_specs, out_specs=out_specs, scratch_shapes=scratch
        ),
        compiler_params=pltpu.CompilerParams(vmem_limit_bytes=48 * 1024 * 1024),
    )


def shape(*dims):
    return jax.ShapeDtypeStruct(dims, BF)


def whole(value):
    return pl.BlockSpec(value.shape, lambda *_: (0,) * len(value.shape))


def columns_of(rows, tile):
    return pl.BlockSpec((rows, tile), lambda j, y: (0, j))


def shift(value, steps):
    return lax.ppermute(value, "y", [(i, (i + steps) % GROUP) for i in range(GROUP)])


def shifts(pieces):
    return [shift(pieces[k - 1], k) for k in range(1, GROUP)]


def spread(value):
    return [shift(value, k) for k in range(1, GROUP)]


def exchange(value):
    return lax.all_to_all(value, ("x", "z"), split_axis=0, concat_axis=0, tiled=True)


def packed(ids, gates):
    high = lax.reduce_precision(gates, 8, 7)
    middle = lax.reduce_precision(gates - high, 8, 7)
    return jnp.concatenate([ids.astype(F32), high, middle, gates - high - middle], axis=-1).astype(BF)


def unpacked(columns):
    top = columns.shape[-1] // 4
    columns = [columns[:, i * top : (i + 1) * top].astype(F32) for i in range(4)]
    return columns[0].astype(jnp.int32), (columns[1] + columns[2]) + columns[3]


def keys(ids, before, place):
    named = [ids[:, k : k + 1] == jnp.arange(LANES, dtype=jnp.int32) for k in range(ids.shape[1])]
    chose = functools.reduce(jnp.logical_or, named)
    rank = dot(before, chose.astype(BF))
    return jnp.where(chose, rank + place, -1.0).astype(BF), named


def expert_rows(per_expert):
    return np.asarray(np.arange(EXPERTS * per_expert)[:, None] // per_expert == np.arange(LANES), dtype=BF)


def codes(places):
    return np.asarray([STRIDE * place + c for _ in range(EXPERTS) for place in places for c in range(CAP)], np.float32)


def unfold(y, pick, value):
    rows, half = pick.shape[1] // 2, value.shape[1]

    def kernel(y_ref, pick_ref, value_ref, *refs):
        joined = dot(pick_ref[0], value_ref[...]).astype(BF)
        for i in range(2):
            refs[i][...] = joined[i * rows : (i + 1) * rows]

    return call(
        kernel,
        [shape(rows, 2 * half)] * 2,
        (2,),
        [pl.BlockSpec((1,) + pick.shape[1:], lambda h, y: (h, 0, 0)), whole(value)],
        [columns_of(rows, half)] * 2,
    )(y, pick, value)


def section_of(here, role):
    return lax.rem(here[1] + 1 - role, 2)


def quarters(y, down, role, runs):
    depth, part = down.shape[2], down.shape[3] // GROUP // runs
    count = (GROUP - 1) * runs

    def kernel(y_ref, down_ref, *refs):
        for i in range(count):

            @pl.when(pl.program_id(0) == i)
            def _():
                refs[i][...] = down_ref[0, 0]

    def column(i, y):
        return (0, section_of(y, role), 0, lax.rem(y[0] + i // runs + 1, GROUP) * runs + lax.rem(i, runs))

    cuts = call(
        kernel,
        [shape(depth, part)] * count,
        (count,),
        [pl.BlockSpec((1, 1, depth, part), column)],
        [pl.BlockSpec((depth, part), lambda k, y: (0, 0))] * count,
    )(y, down)
    return [cuts[run::runs] for run in range(runs)]


def hidden_of(y, rows, gate, up, role):
    width, block = gate.shape[2:]
    total = sum(run.shape[0] for run in rows)
    tile = 1024
    steps = width // tile

    def kernel(y_ref, gate_ref, up_ref, *refs):
        *runs, out_ref, gate_sum, up_sum = refs
        step = pl.program_id(0)

        @pl.when(step == 0)
        def _():
            gate_sum[...] = jnp.zeros_like(gate_sum)
            up_sum[...] = jnp.zeros_like(up_sum)

        value = jnp.concatenate([run[...] for run in runs], axis=0) if len(runs) > 1 else runs[0][...]
        gate_sum[...] += dot(value, gate_ref[0, 0])
        up_sum[...] += dot(value, up_ref[0, 0])

        @pl.when(step == steps - 1)
        def _():
            out_ref[...] = (jax.nn.silu(gate_sum[...]) * up_sum[...]).astype(BF)

    weights = pl.BlockSpec((1, 1, tile, block), lambda j, y: (0, section_of(y, role), j, 0))
    return call(
        kernel,
        shape(total, block),
        (steps,),
        [weights, weights] + [columns_of(run.shape[0], tile) for run in rows],
        pl.BlockSpec((total, block), lambda j, y: (0, 0)),
        [pltpu.VMEM((total, block), F32)] * 2,
        moved=400 * 2**20,
    )(y, gate, up, *rows)


def arrange(y, target, pieces):
    block = pieces[0].shape[1]
    rows = target.shape[1]

    def kernel(y_ref, target_ref, *refs):
        stacked = jnp.concatenate([ref[...] for ref in refs[:-1]], axis=0)
        moved = lax.broadcasted_iota(jnp.int32, (rows, rows), 0) == target_ref[...]
        refs[-1][...] = dot(moved.astype(F32).astype(BF), stacked).astype(BF)

    return call(
        kernel,
        shape(rows, block),
        (1,),
        [whole(target)] + [whole(piece) for piece in pieces],
        pl.BlockSpec((rows, block), lambda j, y: (0, 0)),
    )(y, target, *pieces)


def project(y, units, parts, down, role, moved):
    rows, depth = units[0].shape
    part = sum(group[0].shape[1] for group in parts)
    tile = part // 2
    runs = len(parts)
    flat = [value for group in parts for value in group]

    def kernel(y_ref, *refs):
        *refs, out_ref, joined = refs
        step = pl.program_id(0)

        @pl.when(step == 0)
        def _():
            for k in range(GROUP):
                joined[:, k * depth : (k + 1) * depth] = refs[k][...]

        own, others = refs[GROUP], refs[GROUP + 1 :]
        for run in range(runs):

            @pl.when(step // (2 // runs) == run)
            def _():
                mine = others[run * (GROUP - 1) : (run + 1) * (GROUP - 1)]
                matrix = jnp.concatenate([own[0, 0], *(ref[...] for ref in mine)], axis=0)
                out_ref[...] = dot(joined[...], matrix).astype(BF)

    own = pl.BlockSpec((1, 1, depth, tile), lambda j, y: (0, section_of(y, role), 0, y[0] * 2 + j))
    others = [columns_of(depth, tile) if runs == 1 else whole(value) for value in flat]
    out = call(
        kernel,
        shape(rows, part),
        (2,),
        [whole(unit) for unit in units] + [own] + others,
        columns_of(rows, tile),
        [pltpu.VMEM((rows, GROUP * depth), BF)],
        moved=moved,
    )(y, *units, down, *flat)
    return out.reshape(EXPERTS, GROUP * CAP, part)


def combine(here, back, key, weight, rows=()):
    part, tile = back.shape[2], 896
    back = back.reshape(-1, part)
    tokens = key.shape[0] // GROUP
    onehot = expert_rows(GROUP * CAP)
    code = codes(range(GROUP))[None]
    high = lax.reduce_precision(weight, 8, 7)
    weights = [high.astype(BF), (weight - high).astype(BF)]
    given = len(rows)

    def kernel(here_ref, key_ref, high_ref, low_ref, onehot_ref, code_ref, back_ref, *refs):
        expand = onehot_ref[...]
        hit = dot_t(key_ref[...], expand) == code_ref[...]
        total = 0.0
        for ref in (high_ref, low_ref):
            mix = jnp.where(hit, dot_t(ref[...], expand), 0.0).astype(BF)
            total += dot(mix, back_ref[...])
        for k in range(GROUP):
            piece = total[k * tokens : (k + 1) * tokens]
            if given:
                piece = piece + refs[k][...].astype(F32)
            refs[given + k][...] = piece.astype(BF)

    own = pl.BlockSpec((tokens, tile), lambda j, here: (0, here[0] * (part // tile) + j))
    return call(
        kernel,
        [shape(tokens, part)] * GROUP,
        (part // tile,),
        [whole(value) for value in (key, *weights, onehot, code)] + [columns_of(back.shape[0], tile)] + [own] * given,
        [columns_of(tokens, tile)] * GROUP,
    )(here, key, *weights, onehot, code, back, *rows)


def home(here, totals, rows):
    pieces = [totals[0], *shifts(totals[1:])]
    tokens, part = totals[0].shape

    def kernel(here_ref, rows_ref, *refs):
        for k in range(GROUP):

            @pl.when(pl.program_id(0) == k)
            def _():
                refs[-1][...] = (rows_ref[...].astype(F32) + refs[k][...].astype(F32)).astype(BF)

    quarter = pl.BlockSpec((tokens, part), lambda k, here: (0, lax.rem(here[0] + GROUP - k, GROUP)))
    return call(
        kernel,
        shape(*rows.shape),
        (GROUP,),
        [quarter] + [whole(piece) for piece in pieces],
        quarter,
    )(here, rows, *pieces)


def send(pieces, ranks, size):
    return [
        lax.ppermute(
            pieces[k],
            ("pipe", "y"),
            [(p * GROUP + i, q * GROUP + (i + k) % GROUP) for p, q in ranks for i in range(GROUP)],
        )
        for k in range(size)
    ]


def settle(here, last, ahead, own, late):
    tokens, part = late[0].shape

    def kernel(here_ref, ahead_ref, own_ref, *refs):
        *refs, out_ref = refs
        rank = here_ref[1]
        odd, edge = lax.rem(rank, 2) == 1, jnp.logical_or(rank == 0, rank == last)
        for k in range(GROUP):

            @pl.when(pl.program_id(0) == k)
            def _():
                early, piece = jnp.where(edge, own_ref[...], ahead_ref[...]), refs[k][...]
                out_ref[0] = jnp.where(odd, piece, early)
                out_ref[1] = jnp.where(odd, early, piece)

    def column(k, here):
        return lax.rem(here[0] + GROUP - k, GROUP)

    quarter = pl.BlockSpec((tokens, part), lambda k, here: (0, column(k, here)))
    return call(
        kernel,
        shape(2, *own.shape),
        (GROUP,),
        [quarter] * 2 + [whole(piece) for piece in late],
        pl.BlockSpec((2, tokens, part), lambda k, here: (0, 0, column(k, here))),
    )(here, ahead, own, *late)


def local(activations, expert_ids, gate_values, gate_weight, up_weight, down_weight):
    tokens, width = activations.shape[2:]
    top = expert_ids.shape[3]
    half = width // 2
    index = lax.axis_index("y").astype(jnp.int32)
    rank = lax.axis_index("pipe").astype(jnp.int32)
    y = jnp.stack([index, rank])
    odd = jnp.bitwise_and(rank, 1) == 1

    def roles(value):
        return jnp.where(odd, value[0, 0], value[0, 1]), jnp.where(odd, value[0, 1], value[0, 0])

    first_rows, second_rows = roles(activations)
    ids, gates = roles(expert_ids), roles(gate_values)

    before = np.asarray(np.tril(np.ones((tokens, tokens)), -1), dtype=BF)
    key, _ = keys(ids[0], before, 0.0)
    key = jnp.concatenate([key, jnp.where(key < 0, key, key + STRIDE)], axis=0)
    choose = (dot_t(expert_rows(2 * CAP), key) == codes(range(2))[:, None]).astype(BF)
    halves = jnp.concatenate([first_rows[:, :half], first_rows[:, half:]], axis=0)
    outgoing = dot(choose, halves).astype(BF).reshape(EXPERTS, 2 * CAP, half)
    routing = [packed(ids[s], gates[s]) for s in range(2)]
    routing = jnp.concatenate([*routing, jnp.zeros((tokens, LANES - 8 * top), BF)], axis=1)
    arrived = exchange(outgoing)

    near = spread(second_rows)
    routing = jnp.concatenate([routing, *spread(routing)], axis=0)
    order = np.arange(EXPERTS * CAP)
    source = order // CAP * 2 * CAP + order % CAP + np.arange(2)[:, None] * CAP
    pick = np.asarray(source[:, :, None] == np.arange(EXPERTS * 2 * CAP), dtype=BF)
    arrived = unfold(y, pick, arrived.reshape(EXPERTS * 2 * CAP, half))
    (cuts0,), (cuts1,) = [quarters(y, down_weight, s, 1) for s in range(2)]

    owner = jnp.bitwise_and(index - np.arange(GROUP * tokens, dtype=np.int32)[:, None] // tokens, GROUP - 1)
    before = np.asarray(np.kron(np.eye(GROUP), np.tril(np.ones((tokens, tokens)), -1)), dtype=BF)
    key, weight = [], []
    for s in range(2):
        their_ids, their_gates = unpacked(routing[:, 4 * top * s : 4 * top * (s + 1)])
        found, named = keys(their_ids, before, (owner * STRIDE).astype(F32))
        key.append(found)
        weight.append(sum(jnp.where(named[k], their_gates[:, k : k + 1], 0.0) for k in range(top)))
    onehot = expert_rows(GROUP * CAP)
    choose = (dot_t(onehot, key[1]) == codes(range(GROUP))[:, None]).astype(BF)
    turned = [slice(k * tokens, (k + 1) * tokens) for k in (0, 3, 2, 1)]
    key, weight = [[jnp.concatenate([value[cut] for cut in turned]) for value in group] for group in (key, weight)]
    choose, key0, key1, weight0, weight1 = tie([choose, *key, *weight], [*arrived, *near])

    chosen = dot(choose, jnp.concatenate([second_rows, *near], axis=0)).astype(BF)
    chosen = exchange(chosen.reshape(EXPERTS, GROUP * CAP, width))

    ahead, back = [[shift(run, steps) for run in arrived] for steps in (1, -1)]
    weights = (gate_weight, up_weight)
    far = [shift(ahead[0], 1), shift(back[1], -1)]
    both = hidden_of(y, [*arrived, *ahead, *back], *weights, 0)
    opposite = shift(cuts0[1], 2)
    cut1, cut3, *cuts1 = tie([cuts0[0], cuts0[2], *cuts1], [*far, both, opposite])

    parts0 = [shift(cut1, 1), opposite, shift(cut3, 3)]
    rows = np.arange(EXPERTS * CAP)
    target = np.tile((rows // CAP * GROUP * CAP + rows % CAP).astype(np.int32), GROUP)[None]
    step = np.repeat(np.asarray([0, 1, 3, 2], np.int32), EXPERTS * CAP)[None]
    far_piece = hidden_of(y, far, *weights, 0)
    hidden = arrange(y, target + jnp.bitwise_and(index - step + GROUP, GROUP - 1) * CAP, [both, far_piece])
    units = spread(hidden)
    cuts1 = tie(cuts1, [*units, *parts0])
    units = [hidden, *units]

    parts1 = shifts(cuts1)
    out = project(y, units, [parts0], down_weight, 0, 0)
    (here,) = tie([y], [out.reshape(-1, out.shape[2])])
    hidden_second = hidden_of(here, [chosen.reshape(-1, width)], *weights, 1)
    units_second = [hidden_second, *spread(hidden_second)]
    back0 = exchange(out)
    out = project(y, units_second, [parts1], down_weight, 1, 0)
    out, key0 = tie([out, key0], [])
    back1 = exchange(out)
    result0 = home(y, combine(y, back0, key0, weight0), first_rows)
    size = lax.axis_size("pipe")
    ahead = lax.ppermute(result0, "pipe", [(p, p + 1) for p in range(1, size - 1, 2)] + [(p + 1, p) for p in range(1, size - 1, 2)])
    turned = [second_rows, near[2], near[1], near[0]]
    late = send(combine(y, back1, key1, weight1, turned), [(p, p ^ 1) for p in range(size)], GROUP)
    return settle(y, size - 1, ahead, result0, late)[None]


def solution(mesh):
    pipe = mesh.devices.shape[0]
    split = Mesh(mesh.devices.reshape(pipe, 4, 2, GROUP), ("pipe", "x", "z", "y"))
    wide = ("x", "z", "y")
    return jax.shard_map(
        local,
        mesh=split,
        in_specs=(
            P("pipe", None, wide, None),
            P("pipe", None, wide, None),
            P("pipe", None, wide, None),
            P("pipe", None, None, wide),
            P("pipe", None, None, wide),
            P("pipe", None, wide, None),
        ),
        out_specs=P("pipe", None, wide, None),
        check_vma=False,
    )
```

```python
import functools

import jax
import jax.numpy as jnp
import numpy as np
from jax import lax
from jax.experimental import pallas as pl
from jax.experimental.pallas import tpu as pltpu
from jax.sharding import Mesh, PartitionSpec as P

EXPERTS = 8
CAP = 20
GROUP = 4
PAIR = 2
LANES = 128
STRIDE = 64
BF = jnp.bfloat16
F32 = jnp.float32


def dot(a, b):
    return jnp.dot(a, b, preferred_element_type=F32)


def dot_t(a, b):
    return lax.dot_general(a, b, (((1,), (1,)), ((), ())), preferred_element_type=F32)


def tie(values, earlier):
    anywhere = pl.BlockSpec(memory_space=pl.ANY)
    corner = pl.BlockSpec((16, LANES), lambda i: (0, 0))
    return pl.pallas_call(
        lambda *refs: None,
        out_shape=[jax.ShapeDtypeStruct(value.shape, value.dtype) for value in values],
        in_specs=[anywhere] * len(values) + [corner] * len(earlier),
        out_specs=[anywhere] * len(values),
        grid=(1,),
        input_output_aliases={i: i for i in range(len(values))},
    )(*values, *earlier)


def call(kernel, out_shape, grid, in_specs, out_specs, scratch=(), moved=0):
    return pl.pallas_call(
        kernel,
        cost_estimate=pl.CostEstimate(flops=moved * 500, transcendentals=0, bytes_accessed=moved),
        out_shape=out_shape,
        grid_spec=pltpu.PrefetchScalarGridSpec(
            num_scalar_prefetch=1, grid=grid, in_specs=in_specs, out_specs=out_specs, scratch_shapes=scratch
        ),
        compiler_params=pltpu.CompilerParams(vmem_limit_bytes=48 * 1024 * 1024),
    )


def shape(*dims):
    return jax.ShapeDtypeStruct(dims, BF)


def whole(value):
    return pl.BlockSpec(value.shape, lambda *_: (0,) * len(value.shape))


def columns_of(rows, tile):
    return pl.BlockSpec((rows, tile), lambda j, y: (0, j))


def shift(value, steps):
    return lax.ppermute(value, "y", [(i, (i + steps) % GROUP) for i in range(GROUP)])


def shifts(pieces):
    return [shift(pieces[k - 1], k) for k in range(1, GROUP)]


def spread(value):
    return [shift(value, k) for k in range(1, GROUP)]


def exchange(value):
    return lax.all_to_all(value, ("x", "z"), split_axis=0, concat_axis=0, tiled=True)


def packed(ids, gates):
    high = lax.reduce_precision(gates, 8, 7)
    middle = lax.reduce_precision(gates - high, 8, 7)
    return jnp.concatenate([ids.astype(F32), high, middle, gates - high - middle], axis=-1).astype(BF)


def unpacked(columns):
    top = columns.shape[-1] // 4
    columns = [columns[:, i * top : (i + 1) * top].astype(F32) for i in range(4)]
    return columns[0].astype(jnp.int32), (columns[1] + columns[2]) + columns[3]


def keys(ids, before, place):
    named = [ids[:, k : k + 1] == jnp.arange(LANES, dtype=jnp.int32) for k in range(ids.shape[1])]
    chose = functools.reduce(jnp.logical_or, named)
    rank = dot(before, chose.astype(BF))
    return jnp.where(chose, rank + place, -1.0).astype(BF), named


def expert_rows(per_expert):
    return np.asarray(np.arange(EXPERTS * per_expert)[:, None] // per_expert == np.arange(LANES), dtype=BF)


def codes(places):
    return np.asarray([STRIDE * place + c for _ in range(EXPERTS) for place in places for c in range(CAP)], np.float32)


def unfold(y, pick, value):
    rows, half = pick.shape[1] // 2, value.shape[1]

    def kernel(y_ref, pick_ref, value_ref, *refs):
        joined = dot(pick_ref[0], value_ref[...]).astype(BF)
        for i in range(2):
            refs[i][...] = joined[i * rows : (i + 1) * rows]

    return call(
        kernel,
        [shape(rows, 2 * half)] * 2,
        (2,),
        [pl.BlockSpec((1,) + pick.shape[1:], lambda h, y: (h, 0, 0)), whole(value)],
        [columns_of(rows, half)] * 2,
    )(y, pick, value)


def section_of(here, role):
    return lax.rem(here[1] + 1 - role, 2)


def quarters(y, down, role, runs):
    depth, part = down.shape[2], down.shape[3] // GROUP // runs
    count = (GROUP - 1) * runs

    def kernel(y_ref, down_ref, *refs):
        for i in range(count):

            @pl.when(pl.program_id(0) == i)
            def _():
                refs[i][...] = down_ref[0, 0]

    def column(i, y):
        return (0, section_of(y, role), 0, lax.rem(y[0] + i // runs + 1, GROUP) * runs + lax.rem(i, runs))

    cuts = call(
        kernel,
        [shape(depth, part)] * count,
        (count,),
        [pl.BlockSpec((1, 1, depth, part), column)],
        [pl.BlockSpec((depth, part), lambda k, y: (0, 0))] * count,
    )(y, down)
    return [cuts[run::runs] for run in range(runs)]


def hidden_of(y, rows, gate, up, role):
    width, block = gate.shape[2:]
    total = sum(run.shape[0] for run in rows)
    tile = 1024
    steps = width // tile

    def kernel(y_ref, gate_ref, up_ref, *refs):
        *runs, out_ref, gate_sum, up_sum = refs
        step = pl.program_id(0)

        @pl.when(step == 0)
        def _():
            gate_sum[...] = jnp.zeros_like(gate_sum)
            up_sum[...] = jnp.zeros_like(up_sum)

        value = jnp.concatenate([run[...] for run in runs], axis=0) if len(runs) > 1 else runs[0][...]
        gate_sum[...] += dot(value, gate_ref[0, 0])
        up_sum[...] += dot(value, up_ref[0, 0])

        @pl.when(step == steps - 1)
        def _():
            out_ref[...] = (jax.nn.silu(gate_sum[...]) * up_sum[...]).astype(BF)

    weights = pl.BlockSpec((1, 1, tile, block), lambda j, y: (0, section_of(y, role), j, 0))
    return call(
        kernel,
        shape(total, block),
        (steps,),
        [weights, weights] + [columns_of(run.shape[0], tile) for run in rows],
        pl.BlockSpec((total, block), lambda j, y: (0, 0)),
        [pltpu.VMEM((total, block), F32)] * 2,
        moved=400 * 2**20,
    )(y, gate, up, *rows)


def arrange(y, target, pieces):
    block = pieces[0].shape[1]
    rows = target.shape[1]

    def kernel(y_ref, target_ref, *refs):
        stacked = jnp.concatenate([ref[...] for ref in refs[:-1]], axis=0)
        moved = lax.broadcasted_iota(jnp.int32, (rows, rows), 0) == target_ref[...]
        refs[-1][...] = dot(moved.astype(F32).astype(BF), stacked).astype(BF)

    return call(
        kernel,
        shape(rows, block),
        (1,),
        [whole(target)] + [whole(piece) for piece in pieces],
        pl.BlockSpec((rows, block), lambda j, y: (0, 0)),
    )(y, target, *pieces)


def project(y, units, parts, down, role, moved):
    rows, depth = units[0].shape
    part = sum(group[0].shape[1] for group in parts)
    tile = part // 2
    runs = len(parts)
    flat = [value for group in parts for value in group]

    def kernel(y_ref, *refs):
        *refs, out_ref, joined = refs
        step = pl.program_id(0)

        @pl.when(step == 0)
        def _():
            for k in range(GROUP):
                joined[:, k * depth : (k + 1) * depth] = refs[k][...]

        own, others = refs[GROUP], refs[GROUP + 1 :]
        for run in range(runs):

            @pl.when(step // (2 // runs) == run)
            def _():
                mine = others[run * (GROUP - 1) : (run + 1) * (GROUP - 1)]
                matrix = jnp.concatenate([own[0, 0], *(ref[...] for ref in mine)], axis=0)
                out_ref[...] = dot(joined[...], matrix).astype(BF)

    own = pl.BlockSpec((1, 1, depth, tile), lambda j, y: (0, section_of(y, role), 0, y[0] * 2 + j))
    others = [columns_of(depth, tile) if runs == 1 else whole(value) for value in flat]
    out = call(
        kernel,
        shape(rows, part),
        (2,),
        [whole(unit) for unit in units] + [own] + others,
        columns_of(rows, tile),
        [pltpu.VMEM((rows, GROUP * depth), BF)],
        moved=moved,
    )(y, *units, down, *flat)
    return out.reshape(EXPERTS, GROUP * CAP, part)


def combine(here, back, key, weight, rows=()):
    part, tile = back.shape[2], 896
    back = back.reshape(-1, part)
    tokens = key.shape[0] // GROUP
    onehot = expert_rows(GROUP * CAP)
    code = codes(range(GROUP))[None]
    high = lax.reduce_precision(weight, 8, 7)
    weights = [high.astype(BF), (weight - high).astype(BF)]
    given = len(rows)

    def kernel(here_ref, key_ref, high_ref, low_ref, onehot_ref, code_ref, back_ref, *refs):
        expand = onehot_ref[...]
        hit = dot_t(key_ref[...], expand) == code_ref[...]
        total = 0.0
        for ref in (high_ref, low_ref):
            mix = jnp.where(hit, dot_t(ref[...], expand), 0.0).astype(BF)
            total += dot(mix, back_ref[...])
        for k in range(GROUP):
            piece = total[k * tokens : (k + 1) * tokens]
            if given:
                piece = piece + refs[k][...].astype(F32)
            refs[given + k][...] = piece.astype(BF)

    own = pl.BlockSpec((tokens, tile), lambda j, here: (0, here[0] * (part // tile) + j))
    return call(
        kernel,
        [shape(tokens, part)] * GROUP,
        (part // tile,),
        [whole(value) for value in (key, *weights, onehot, code)] + [columns_of(back.shape[0], tile)] + [own] * given,
        [columns_of(tokens, tile)] * GROUP,
    )(here, key, *weights, onehot, code, back, *rows)


def home(here, totals, rows):
    pieces = [totals[0], *shifts(totals[1:])]
    tokens, part = totals[0].shape

    def kernel(here_ref, rows_ref, *refs):
        for k in range(GROUP):

            @pl.when(pl.program_id(0) == k)
            def _():
                refs[-1][...] = (rows_ref[...].astype(F32) + refs[k][...].astype(F32)).astype(BF)

    quarter = pl.BlockSpec((tokens, part), lambda k, here: (0, lax.rem(here[0] + GROUP - k, GROUP)))
    return call(
        kernel,
        shape(*rows.shape),
        (GROUP,),
        [quarter] + [whole(piece) for piece in pieces],
        quarter,
    )(here, rows, *pieces)


def send(pieces, ranks, size):
    return [
        lax.ppermute(
            pieces[k],
            ("pipe", "y"),
            [(p * GROUP + i, q * GROUP + (i + k) % GROUP) for p, q in ranks for i in range(GROUP)],
        )
        for k in range(size)
    ]


def settle(here, last, ahead, own, late):
    tokens, part = late[0].shape

    def kernel(here_ref, ahead_ref, own_ref, *refs):
        *refs, out_ref = refs
        rank = here_ref[1]
        odd, edge = lax.rem(rank, 2) == 1, jnp.logical_or(rank == 0, rank == last)
        for k in range(GROUP):

            @pl.when(pl.program_id(0) == k)
            def _():
                early, piece = jnp.where(edge, own_ref[...], ahead_ref[...]), refs[k][...]
                out_ref[0] = jnp.where(odd, piece, early)
                out_ref[1] = jnp.where(odd, early, piece)

    def column(k, here):
        return lax.rem(here[0] + GROUP - k, GROUP)

    quarter = pl.BlockSpec((tokens, part), lambda k, here: (0, column(k, here)))
    return call(
        kernel,
        shape(2, *own.shape),
        (GROUP,),
        [quarter] * 2 + [whole(piece) for piece in late],
        pl.BlockSpec((2, tokens, part), lambda k, here: (0, 0, column(k, here))),
    )(here, ahead, own, *late)


def local(activations, expert_ids, gate_values, gate_weight, up_weight, down_weight):
    tokens, width = activations.shape[2:]
    top = expert_ids.shape[3]
    half = width // 2
    index = lax.axis_index("y").astype(jnp.int32)
    rank = lax.axis_index("pipe").astype(jnp.int32)
    y = jnp.stack([index, rank])
    odd = jnp.bitwise_and(rank, 1) == 1

    def roles(value):
        return jnp.where(odd, value[0, 0], value[0, 1]), jnp.where(odd, value[0, 1], value[0, 0])

    first_rows, second_rows = roles(activations)
    ids, gates = roles(expert_ids), roles(gate_values)

    before = np.asarray(np.tril(np.ones((tokens, tokens)), -1), dtype=BF)
    key, _ = keys(ids[0], before, 0.0)
    key = jnp.concatenate([key, jnp.where(key < 0, key, key + STRIDE)], axis=0)
    choose = (dot_t(expert_rows(2 * CAP), key) == codes(range(2))[:, None]).astype(BF)
    halves = jnp.concatenate([first_rows[:, :half], first_rows[:, half:]], axis=0)
    outgoing = dot(choose, halves).astype(BF).reshape(EXPERTS, 2 * CAP, half)
    routing = [packed(ids[s], gates[s]) for s in range(2)]
    routing = jnp.concatenate([*routing, jnp.zeros((tokens, LANES - 8 * top), BF)], axis=1)
    arrived = exchange(outgoing)

    near = spread(second_rows)
    routing = jnp.concatenate([routing, *spread(routing)], axis=0)
    order = np.arange(EXPERTS * CAP)
    source = order // CAP * 2 * CAP + order % CAP + np.arange(2)[:, None] * CAP
    pick = np.asarray(source[:, :, None] == np.arange(EXPERTS * 2 * CAP), dtype=BF)
    arrived = unfold(y, pick, arrived.reshape(EXPERTS * 2 * CAP, half))
    (cuts0,), (cuts1,) = [quarters(y, down_weight, s, 1) for s in range(2)]

    owner = jnp.bitwise_and(index - np.arange(GROUP * tokens, dtype=np.int32)[:, None] // tokens, GROUP - 1)
    before = np.asarray(np.kron(np.eye(GROUP), np.tril(np.ones((tokens, tokens)), -1)), dtype=BF)
    key, weight = [], []
    for s in range(2):
        their_ids, their_gates = unpacked(routing[:, 4 * top * s : 4 * top * (s + 1)])
        found, named = keys(their_ids, before, (owner * STRIDE).astype(F32))
        key.append(found)
        weight.append(sum(jnp.where(named[k], their_gates[:, k : k + 1], 0.0) for k in range(top)))
    onehot = expert_rows(GROUP * CAP)
    choose = (dot_t(onehot, key[1]) == codes(range(GROUP))[:, None]).astype(BF)
    turned = [slice(k * tokens, (k + 1) * tokens) for k in (0, 3, 2, 1)]
    key, weight = [[jnp.concatenate([value[cut] for cut in turned]) for value in group] for group in (key, weight)]
    choose, key0, key1, weight0, weight1 = tie([choose, *key, *weight], [*arrived, *near])

    chosen = dot(choose, jnp.concatenate([second_rows, *near], axis=0)).astype(BF)
    chosen = exchange(chosen.reshape(EXPERTS, GROUP * CAP, width))

    ahead, back = [[shift(run, steps) for run in arrived] for steps in (1, -1)]
    weights = (gate_weight, up_weight)
    far = [shift(ahead[0], 1), shift(back[1], -1)]
    both = hidden_of(y, [*arrived, *ahead, *back], *weights, 0)
    opposite = shift(cuts0[1], 2)
    cut1, cut3, *cuts1 = tie([cuts0[0], cuts0[2], *cuts1], [*far, both, opposite])

    parts0 = [shift(cut1, 1), opposite, shift(cut3, 3)]
    rows = np.arange(EXPERTS * CAP)
    target = np.tile((rows // CAP * GROUP * CAP + rows % CAP).astype(np.int32), GROUP)[None]
    step = np.repeat(np.asarray([0, 1, 3, 2], np.int32), EXPERTS * CAP)[None]
    far_piece = hidden_of(y, far, *weights, 0)
    hidden = arrange(y, target + jnp.bitwise_and(index - step + GROUP, GROUP - 1) * CAP, [both, far_piece])
    units = spread(hidden)
    cuts1 = tie(cuts1, [parts0[0], parts0[2]])
    units = [hidden, *units]

    parts1 = shifts(cuts1)
    out = project(y, units, [parts0], down_weight, 0, 0)
    (here,) = tie([y], [out.reshape(-1, out.shape[2])])
    hidden_second = hidden_of(here, [chosen.reshape(-1, width)], *weights, 1)
    units_second = [hidden_second, *spread(hidden_second)]
    back0 = exchange(out)
    out = project(y, units_second, [parts1], down_weight, 1, 0)
    out, key0 = tie([out, key0], [])
    back1 = exchange(out)
    result0 = home(y, combine(y, back0, key0, weight0), first_rows)
    size = lax.axis_size("pipe")
    ahead = lax.ppermute(result0, "pipe", [(p, p + 1) for p in range(1, size - 1, 2)] + [(p + 1, p) for p in range(1, size - 1, 2)])
    turned = [second_rows, near[2], near[1], near[0]]
    late = send(combine(y, back1, key1, weight1, turned), [(p, p ^ 1) for p in range(size)], GROUP)
    return settle(y, size - 1, ahead, result0, late)[None]


def solution(mesh):
    pipe = mesh.devices.shape[0]
    split = Mesh(mesh.devices.reshape(pipe, 4, 2, GROUP), ("pipe", "x", "z", "y"))
    wide = ("x", "z", "y")
    return jax.shard_map(
        local,
        mesh=split,
        in_specs=(
            P("pipe", None, wide, None),
            P("pipe", None, wide, None),
            P("pipe", None, wide, None),
            P("pipe", None, None, wide),
            P("pipe", None, None, wide),
            P("pipe", None, wide, None),
        ),
        out_specs=P("pipe", None, wide, None),
        check_vma=False,
    )
```
